256 devices in a mesh: shot: 16 (over x, y_lo, core), sub: 16 (over y_hi, z).
Axes of the slice: x: 4, y: 4 (y_hi: 2, y_lo: 2; y = y_hi * 2 + y_lo), z: 8, core: 2. Of those that a mesh axis runs over, the one named last changes fastest.
Arguments:
- field_before: float32 [16, 512, 64, 256], P('shot', 'sub'), may hold values from -6 to 6
- field_now: float32 [16, 512, 64, 256], P('shot', 'sub'), may hold values from -6 to 6
- snapshots: bfloat16 [16, 2, 512, 64, 256], P('shot', None, 'sub'), may hold values from -6 to 6
- traces: float32 [16, 16, 2, 128], P('shot', 'sub'), may hold values from -6 to 6
- receivers: int32 [16, 16, 128], P('shot', 'sub'), may hold values from 65536 to 458751, as said below
- courant: float32 [512, 256, 256], P('sub', 'shot'), may hold values from 0.05 to 0.18
- aperture: int32 [16], replicated, may hold values from 0 to 12
- block_of: int32 [16], replicated, may hold values from 0 to 15, each once
Outputs:
- field_prior: float32 [16, 512, 64, 256], P('shot', 'sub')
- field_final: float32 [16, 512, 64, 256], P('shot', 'sub')
- image: float32 [512, 256, 256], P('sub', 'shot')
The draws below stay inside these ranges and needn't reach their ends.
Inputs may be any that keep to these rules, and one draw needn't show every extreme that they name: `receivers`: each receiver lies at least 4 cells inside its device's part along the first dimension.
All inputs are finite; a program needn't handle non-finite values.
Results may differ from the reference program's by a relative error of at most 0.0003.
Values sent between devices are 32-bit elements; how exact they have to be, the bound alone decides.
A program may use at most 128 MiB of HBM per device.

```python
import math
import jax
import jax.numpy as jnp
from jax import lax

CX = 32
CY = 16
NZ = 256
APY = 4
STEPS = 2
RDEV = 128
AY = 64
NXT = 512
MY = 256
N_SHOT = 16
N_SUB = 16


def draw_receivers(key, part):
    key = jax.random.fold_in(key, 7)
    key_x, key_y, key_z = jax.random.split(key, 3)
    shape = (N_SHOT, N_SUB, RDEV)
    row_x = jax.random.randint(key_x, shape, 4, CX - 4)
    row_y = jax.random.randint(key_y, shape, 0, APY * CY)
    row_z = jax.random.randint(key_z, shape, 0, NZ)
    return ((row_x * (APY * CY) + row_y) * NZ + row_z).astype(jnp.int32)


def set_ends(entries, stream_key, least, largest):
    longest = entries.shape.index(max(entries.shape))
    spots = []
    for shift in (0, 1):
        where = [jax.random.randint(jax.random.fold_in(stream_key, axis), (), 0, length) for axis, length in enumerate(entries.shape)]
        where[longest] = (where[longest] + shift) % entries.shape[longest]
        spots.append(tuple(where))
    return entries.at[spots[0]].set(least).at[spots[1]].set(largest)


def level_of(rng, dims, cuts, smallest, top_value):
    factor_of, own = 1.0, jax.random.fold_in(rng, 6)
    for position, blocks in cuts:
        heights = jnp.exp(jax.random.uniform(jax.random.fold_in(own, position), (blocks,), jnp.float32, smallest / len(cuts), top_value / len(cuts)))
        factor_of = factor_of * jnp.repeat(heights, dims[position] // blocks).reshape([-1 if axis == position else 1 for axis in range(len(dims))])
    return factor_of


def noise(key, dims, spread, reach, cuts=(), kind=jnp.bfloat16):
    drawn = spread * jax.random.normal(key, dims, jnp.float32)
    if cuts:
        drawn = drawn * level_of(key, dims, cuts, -0.22, 0.18)
    return jnp.clip(drawn, -reach, reach).astype(kind)


def setup_inputs(seed: int = 0) -> dict:
    seeds = jax.random.split(jax.random.key(seed), 9)
    field_before = noise(seeds[0], (N_SHOT, NXT, AY, NZ), 1.0, 6.0, ((0, 16), (1, 16)), jnp.float32)
    field_now = noise(seeds[1], (N_SHOT, NXT, AY, NZ), 1.0, 6.0, ((0, 16), (1, 16)), jnp.float32)
    snapshots = noise(seeds[2], (N_SHOT, STEPS, NXT, AY, NZ), 1.0, 6.0, ((0, 16), (2, 16)))
    traces = noise(seeds[3], (N_SHOT, N_SUB, STEPS, RDEV), 1.0, 6.0, ((0, 16), (1, 16)), jnp.float32)
    receivers = draw_receivers(jax.random.fold_in(seeds[8], 71), 0)
    courant = jnp.clip(jnp.exp(math.log(0.18) - 1.2809339 * jax.random.uniform(seeds[5], (NXT, MY, NZ), jnp.float32) ** level_of(seeds[5], (NXT, MY, NZ), ((0, 16), (1, 16)), -0.2, 0.2)), 0.05, 0.18)
    aperture = set_ends(jax.random.randint(seeds[6], (N_SHOT,), 0, N_SHOT - APY + 1), jax.random.fold_in(seeds[6], 1), 0, N_SHOT - APY).astype(jnp.int32)
    block_of = jax.random.permutation(seeds[7], N_SHOT).astype(jnp.int32)
    return {"field_before": field_before, "field_now": field_now, "snapshots": snapshots, "traces": traces, "receivers": receivers, "courant": courant, "aperture": aperture, "block_of": block_of}


centre_weight = -205.0 / 72.0
side_weights = (8.0 / 5.0, -1.0 / 5.0, 8.0 / 315.0, -1.0 / 560.0)


def laplace(extended):
    size_x = extended.shape[0] - 8
    size_y = extended.shape[1]
    size_z = extended.shape[2]
    padded = jnp.pad(extended, ((0, 0), (4, 4), (4, 4)))

    def window(shift_x, shift_y, shift_z):
        return padded[4 + shift_x:4 + shift_x + size_x, 4 + shift_y:4 + shift_y + size_y, 4 + shift_z:4 + shift_z + size_z]

    summed = 3.0 * centre_weight * window(0, 0, 0)
    for distance in range(1, 5):
        weight = side_weights[distance - 1]
        summed = summed + weight * (window(distance, 0, 0) + window(-distance, 0, 0) + window(0, distance, 0) + window(0, -distance, 0) + window(0, 0, distance) + window(0, 0, -distance))
    return summed


def reference(field_before, field_now, snapshots, traces, receivers, courant, aperture, block_of):
    ranks = jnp.arange(N_SHOT, dtype=jnp.int32)
    inverse = jnp.zeros((N_SHOT,), jnp.int32).at[block_of].set(ranks)
    model = courant.reshape(NXT, N_SHOT, CY, NZ)[:, inverse].reshape(NXT, MY, NZ)
    offsets = (jnp.arange(N_SUB, dtype=jnp.int32) * (CX * AY * NZ))[:, None]

    def one_shot(model_image, inputs):
        previous, current, snaps, shot_traces, shot_receivers, first_block = inputs
        anchor = (first_block * CY).astype(jnp.int32)
        zero_index = jnp.zeros((), jnp.int32)
        speed = lax.dynamic_slice(model, (zero_index, anchor, zero_index), (NXT, AY, NZ))
        flat_index = (shot_receivers + offsets).reshape(-1)
        shot_image = jnp.zeros((NXT, AY, NZ), jnp.float32)
        for instant in range(STEPS):
            extended = jnp.pad(current, ((4, 4), (0, 0), (0, 0)))
            advanced = 2.0 * current - previous + speed * laplace(extended)
            advanced = advanced.reshape(-1).at[flat_index].add(shot_traces[:, instant, :].reshape(-1)).reshape(NXT, AY, NZ)
            shot_image = shot_image + snaps[instant].astype(jnp.float32) * advanced
            previous, current = current, advanced
        placed = lax.dynamic_slice(model_image, (zero_index, anchor, zero_index), (NXT, AY, NZ)) + shot_image
        model_image = lax.dynamic_update_slice(model_image, placed, (zero_index, anchor, zero_index))
        return model_image, (previous, current)

    start_image = jnp.zeros((NXT, MY, NZ), jnp.float32)
    model_image, outputs = lax.scan(one_shot, start_image, (field_before, field_now, snapshots, traces, receivers, aperture))
    image = model_image.reshape(NXT, N_SHOT, CY, NZ)[:, block_of].reshape(NXT, MY, NZ)
    return outputs[0], outputs[1], image
```

```python
import functools

import jax
import jax.numpy as jnp
import ml_dtypes
import numpy as np
from jax import lax
from jax.experimental import pallas as pl
from jax.experimental.pallas import tpu as pltpu
from jax.sharding import PartitionSpec as P

MESH = pl.DeviceIdType.MESH
F32 = jnp.float32
BF16 = jnp.bfloat16

NX, NY, NZ, BY, NB, NR = 32, 64, 256, 16, 16, 128
HALO = 4
centre_weight = -205.0 / 72.0
side_weights = (8.0 / 5.0, -1.0 / 5.0, 8.0 / 315.0, -1.0 / 560.0)

CHUNKS = ((0, 8, 2), (8, 8, 3), (16, 8, 3), (24, 8, 2))
ORDER = (0, 3, 1, 2)
OWN, A, B, D = range(4)


def split(value):
    high = value.astype(BF16)
    low = (value - high.astype(F32)).astype(BF16)
    return high, low


def band(i, j):
    apart = jnp.abs(i - j)
    high = jnp.zeros(apart.shape, F32)
    low = jnp.zeros(apart.shape, F32)
    for distance in range(1, 5):
        weight = np.float32(side_weights[distance - 1])
        top = np.float32(weight.astype(ml_dtypes.bfloat16))
        high = jnp.where(apart == distance, float(top), high)
        low = jnp.where(apart == distance, float(weight - top), low)
    return high.astype(BF16), low.astype(BF16)


def kernel(before, now, snapshots, traces, receivers, courant, aperture, block_of,
           prior_out, final_out, image_out,
           fpad, npad, base, lap, last, snap, wz, wy, spots,
           speed, gath, stage, img, imgin, sibout, sibin, acc, xin, yin, imgout,
           send_sems, recv_sems, local_sems):
    s = lax.axis_index("shot")
    u = lax.axis_index("sub")
    c = lax.rem(s, 2)
    y = lax.rem(s // 2, 2)
    x = s // 4
    way = 1 - 2 * c

    def at(x_, y_, c_):
        return {"shot": (x_ * 2 + y_) * 2 + c_, "sub": u}

    def column(role, way_):
        return lax.rem({OWN: x, A: x - way_ + 4, B: x + way_ + 4, D: x + 2}[role], 4)

    dev = {
        "A": at(column(A, way), y, c),
        "B": at(column(B, way), y, c),
        "Y": at(x, 1 - y, c),
        "C": at(x, y, 1 - c),
        "S+": {"shot": s, "sub": lax.rem(u + 1, 16)},
        "S-": {"shot": s, "sub": lax.rem(u + 15, 16)},
    }
    ids = {}
    sent = []

    def number(name):
        return ids.setdefault(name, len(ids))

    def copy_of(name, src, dst, to):
        n = number(name)
        return pltpu.make_async_remote_copy(
            src_ref=src, dst_ref=dst, send_sem=send_sems.at[n], recv_sem=recv_sems.at[n],
            device_id=dev[to], device_id_type=MESH)

    def send(name, src, dst, to):
        copy = copy_of(name, src, dst, to)
        copy.start()
        sent.append(copy)

    def arrive(name, dst):
        copy_of(name, dst, dst, "Y").wait_recv()

    locals_ = {}

    def local(name, src, dst):
        copy = pltpu.make_async_copy(src, dst, local_sems.at[len(locals_)])
        locals_[name] = copy
        copy.start()

    def shape_of(k):
        first, size, h = CHUNKS[k]
        return first, size, h, size - h

    for k in ORDER:
        first, size, h, r = shape_of(k)
        local(("own", k), courant.at[pl.ds(first + y * h, r)], gath[k].at[c * 8 + x * 2 + y])
    for k in (1, 2, 0, 3):
        first, size, h, r = shape_of(k)
        local(("now", k), now.at[0, pl.ds(first, size)], fpad.at[pl.ds(HALO + first, size)])
    for k in (1, 2, 0, 3):
        first, size, h, r = shape_of(k)
        local(("before", k), before.at[0, pl.ds(first, size)], base.at[pl.ds(first, size)])
    local("snap", snapshots.at[0], snap)

    barrier = pltpu.get_barrier_semaphore()
    for name in dev:
        pl.semaphore_signal(barrier, inc=1, device_id=dev[name], device_id_type=MESH)
    pl.semaphore_wait(barrier, len(dev))

    def halo_send(name, up_src, down_src, pad):
        up = copy_of(name + "up", up_src, pad.at[pl.ds(0, HALO)], "S+")
        down = copy_of(name + "down", down_src, pad.at[pl.ds(HALO + NX, HALO)], "S-")

        @pl.when(u < 15)
        def _():
            up.start()

        @pl.when(u > 0)
        def _():
            down.start()

        return up, down

    def halo_low(copies):
        @pl.when(u > 0)
        def _():
            copies[0].wait_recv()

    def halo_high(copies):
        @pl.when(u < 15)
        def _():
            copies[1].wait_recv()

    def halo_sent(copies):
        @pl.when(u < 15)
        def _():
            copies[0].wait_send()

        @pl.when(u > 0)
        def _():
            copies[1].wait_send()

    def pair(role, c_):
        return pl.ds(c_ * 8 + 2 * column(role, 1 - 2 * c_), 2)

    def gather_y(k):
        first, size, h, r = shape_of(k)
        send(("gy", k), courant.at[pl.ds(first + (1 - y) * h, r)], gath[k].at[c * 8 + x * 2 + y], "Y")

    def gather_x(k):
        arrive(("gy", k), gath[k].at[c * 8 + x * 2 + 1 - y])
        locals_[("own", k)].wait()
        mine = gath[k].at[pair(OWN, c)]
        send(("ga", k), mine, mine, "A")
        send(("gb", k), mine, mine, "B")
        send(("gc", OWN, k), mine, mine, "C")

    def gather_forward(k):
        from_a = gath[k].at[pair(A, c)]
        arrive(("gb", k), from_a)
        send(("gd", k), from_a, from_a, "B")
        send(("gc", A, k), from_a, from_a, "C")

    def gather_sibling(k):
        from_b = gath[k].at[pair(B, c)]
        arrive(("ga", k), from_b)
        send(("gc", B, k), from_b, from_b, "C")
        from_d = gath[k].at[pair(D, c)]
        arrive(("gd", k), from_d)
        send(("gc", D, k), from_d, from_d, "C")

    def slots_from(first_block):
        found = []
        for j in range(4):
            slot = 0
            for b in range(NB):
                slot = jnp.where(block_of[b] == first_block + j, (b % 2) * 8 + b // 2, slot)
            found.append(slot)
        return found

    def gather_stage(k):
        first, size, h, r = shape_of(k)
        for role in (OWN, A, B, D):
            arrive(("gc", role, k), gath[k].at[pair(role, 1 - c)])
        for j in range(4):
            stage[k][:, BY * j:BY * j + BY, :] = gath[k][their_slots[j], pl.ds(y * (r - h), h)]
        send(("gs", k), stage[k], speed[k].at[pl.ds(y * r, h)], "Y")
        for j in range(4):
            speed[k][pl.ds(y * h, r), BY * j:BY * j + BY, :] = gath[k][my_slots[j]]

    def matrices():
        i = lax.broadcasted_iota(jnp.int32, (256, 256), 0)
        j = lax.broadcasted_iota(jnp.int32, (256, 256), 1)
        high, low = band(i, j)
        wz[0:256, :] = high
        wz[256:512, :] = high
        wz[512:768, :] = low
        same = (i // NY) == (j // NY)
        high = jnp.where(same, high.astype(F32), 0.0).astype(BF16)
        low = jnp.where(same, low.astype(F32), 0.0).astype(BF16)
        wy[:, 0:256] = high
        wy[:, 256:512] = high
        wy[:, 512:768] = low

    def depth_spots():
        z = lax.broadcasted_iota(jnp.int32, (NZ, NR), 0)
        at_depth = z == lax.rem(receivers[0], NZ)
        for t in range(2):
            value = jnp.where(at_depth, traces[0, 0, t:t + 1, :], 0.0)
            high = value.astype(BF16)
            rest = value - high.astype(F32)
            middle = rest.astype(BF16)
            low = (rest - middle.astype(F32)).astype(BF16)
            spots[t, :, 0:NR] = high
            spots[t, :, NR:2 * NR] = middle
            spots[t, :, 2 * NR:3 * NR] = low

    def injected(layer, t):
        row = lax.broadcasted_iota(jnp.int32, (4 * NY, NR), 0) + layer * NY
        hit = jnp.where(row == receivers[0] // NZ, 1.0, 0.0).astype(BF16)
        hits = jnp.concatenate([hit, hit, hit], axis=1)
        return lax.dot_general(hits, spots[t], (((1,), (1,)), ((), ())), preferred_element_type=F32)

    def laplace(pad, layer):
        field = pad[pl.ds(layer + HALO, 4)]
        rows = field.reshape(4 * NY, NZ)
        high, low = split(rows)
        summed = jnp.dot(jnp.concatenate([high, low, high], axis=1), wz[...], preferred_element_type=F32)
        summed = summed + jnp.dot(wy[...], jnp.concatenate([high, low, high], axis=0), preferred_element_type=F32)
        summed = summed.reshape(4, NY, NZ) + (3.0 * centre_weight) * field
        for distance in range(1, 5):
            summed = summed + side_weights[distance - 1] * (
                pad[pl.ds(layer + HALO + distance, 4)] + pad[pl.ds(layer + HALO - distance, 4)])
        return field, summed

    def groups(k, body):
        first, size, h, r = shape_of(k)

        def step(g, carry):
            body(first + 4 * g, 4 * g)
            return carry

        lax.fori_loop(0, size // 4, step, 0)

    def prepare(k):
        locals_[("before", k)].wait()

        def body(layer, inside):
            field, summed = laplace(fpad, layer)
            lap[pl.ds(layer, 4)] = summed
            base[pl.ds(layer, 4)] = (2.0 * field - base[pl.ds(layer, 4)]
                                     + injected(layer, 0).reshape(4, NY, NZ))

        groups(k, body)

    def step_one(k):
        first, size, h, r = shape_of(k)
        arrive(("gs", k), speed[k].at[pl.ds((1 - y) * r, h)])

        def body(layer, inside):
            npad[pl.ds(layer + HALO, 4)] = (base[pl.ds(layer, 4)]
                                            + speed[k][pl.ds(inside, 4)] * lap[pl.ds(layer, 4)])

        groups(k, body)
        local(("prior", k), npad.at[pl.ds(HALO + first, size)], prior_out.at[0, pl.ds(first, size)])

    def step_two(k):
        first, size, h, r = shape_of(k)

        def body(layer, inside):
            field, summed = laplace(npad, layer)
            value = (2.0 * field - fpad[pl.ds(layer + HALO, 4)] + speed[k][pl.ds(inside, 4)] * summed
                     + injected(layer, 1).reshape(4, NY, NZ))
            last[pl.ds(layer, 4)] = value
            seen = snap[0, pl.ds(layer, 4)].astype(F32) * field + snap[1, pl.ds(layer, 4)].astype(F32) * value
            for j in range(4):
                img[k][j, pl.ds(inside, 4)] = seen[:, BY * j:BY * j + BY, :]

        groups(k, body)
        local(("final", k), last.at[pl.ds(first, size)], final_out.at[0, pl.ds(first, size)])
        img[k][4] = jnp.zeros((size, BY, NZ), F32)
        imgin[k][4] = jnp.zeros((h, BY, NZ), F32)
        send(("ry", k), img[k].at[pl.ds(0, 4), pl.ds((1 - y) * r, h)], imgin[k].at[pl.ds(0, 4)], "Y")

    def place(first_block, storage):
        block = block_of[storage] - first_block
        return jnp.where((block >= 0) & (block < 4), block, 4)

    def reduce_sibling(k):
        first, size, h, r = shape_of(k)
        arrive(("ry", k), imgin[k].at[pl.ds(0, 4)])
        for to, core in ((sibout[k], 1 - c), (acc[k], c)):
            def body(slot, carry, to=to, core=core):
                storage = 2 * slot + core
                to[slot] = img[k][place(my_first, storage), pl.ds(y * h, r)]
                inner = pl.ds(y * (r - h), h)
                to[slot, inner] = to[slot, inner] + imgin[k][place(their_first, storage)]
                return carry

            lax.fori_loop(0, 8, body, 0)
            if to is sibout[k]:
                send(("rc", k), sibout[k], sibin[k], "C")

    def reduce_x(k):
        arrive(("rc", k), sibin[k])

        def body(slot, carry):
            acc[k][slot] = acc[k][slot] + sibin[k][slot]
            return carry

        lax.fori_loop(0, 8, body, 0)
        send(("rd", k), acc[k].at[pl.ds(2 * column(D, way), 2)], xin[k].at[0], "B")
        send(("ra", k), acc[k].at[pl.ds(2 * column(A, way), 2)], xin[k].at[1], "A")

    def reduce_forward(k):
        arrive(("rd", k), xin[k].at[0])
        to_b = pl.ds(2 * column(B, way), 2)
        acc[k][to_b] = acc[k][to_b] + xin[k][0]
        send(("rb", k), acc[k].at[to_b], xin[k].at[2], "B")

    def reduce_y(k):
        arrive(("ra", k), xin[k].at[1])
        arrive(("rb", k), xin[k].at[2])
        mine = pl.ds(2 * x, 2)
        acc[k][mine] = acc[k][mine] + xin[k][1] + xin[k][2]
        send(("rz", k), acc[k].at[2 * x + 1 - y], yin[k], "Y")

    def finish(k):
        first, size, h, r = shape_of(k)
        arrive(("rz", k), yin[k])
        imgout[k][...] = jnp.zeros((size, BY, NZ), F32)
        imgout[k][pl.ds(y * h, r)] = acc[k][2 * x + y]
        theirs = pl.ds((1 - y) * h, r)
        imgout[k][theirs] = imgout[k][theirs] + yin[k][...]
        local(("image", k), imgout[k], image_out.at[pl.ds(first, size)])

    for k in ORDER:
        gather_y(k)
    first_halo = halo_send("h0", now.at[0, pl.ds(NX - HALO, HALO)], now.at[0, pl.ds(0, HALO)], fpad)

    @pl.when(u == 0)
    def _():
        fpad[0:HALO] = jnp.zeros((HALO, NY, NZ), F32)
        npad[0:HALO] = jnp.zeros((HALO, NY, NZ), F32)

    @pl.when(u == 15)
    def _():
        fpad[HALO + NX:] = jnp.zeros((HALO, NY, NZ), F32)
        npad[HALO + NX:] = jnp.zeros((HALO, NY, NZ), F32)

    my_first = aperture[s]
    their_first = aperture[(x * 2 + 1 - y) * 2 + c]
    my_slots = slots_from(my_first)
    their_slots = slots_from(their_first)
    matrices()
    depth_spots()
    gather_x(0)
    gather_x(3)
    for k in (1, 2, 0, 3):
        locals_[("now", k)].wait()
    prepare(1)
    gather_forward(0)
    gather_x(1)
    prepare(2)
    gather_sibling(0)
    gather_forward(3)
    gather_x(2)
    halo_low(first_halo)
    prepare(0)
    gather_stage(0)
    halo_high(first_halo)
    prepare(3)
    gather_sibling(3)
    gather_forward(1)
    gather_stage(3)
    step_one(0)
    gather_sibling(1)
    gather_forward(2)
    gather_stage(1)
    step_one(3)
    second_halo = halo_send("h1", npad.at[pl.ds(NX, HALO)], npad.at[pl.ds(HALO, HALO)], npad)
    locals_["snap"].wait()
    gather_sibling(2)
    gather_stage(2)
    step_one(1)
    halo_low(second_halo)
    step_two(0)
    step_one(2)
    halo_high(second_halo)
    step_two(3)
    reduce_sibling(0)
    step_two(1)
    reduce_x(0)
    reduce_sibling(3)
    step_two(2)
    reduce_forward(0)
    reduce_x(3)
    reduce_sibling(1)
    reduce_y(0)
    reduce_forward(3)
    reduce_x(1)
    reduce_sibling(2)
    finish(0)
    reduce_y(3)
    reduce_forward(1)
    reduce_x(2)
    finish(3)
    reduce_y(1)
    reduce_forward(2)
    finish(1)
    reduce_y(2)
    finish(2)

    halo_sent(first_halo)
    halo_sent(second_halo)
    for copy in sent:
        copy.wait_send()
    for name in locals_:
        if name[0] in ("prior", "final", "image"):
            locals_[name].wait()


def local(field_before, field_now, snapshots, traces, receivers, courant, aperture, block_of):
    anywhere = pl.BlockSpec(memory_space=pl.ANY)
    vector = pl.BlockSpec(memory_space=pltpu.VMEM)
    scalar = pl.BlockSpec(memory_space=pltpu.SMEM)

    def per_chunk(dims):
        return [pltpu.VMEM(dims(size, h, size - h), F32) for first, size, h in CHUNKS]

    field = (NX, NY, NZ)
    padded = (NX + 2 * HALO, NY, NZ)
    block = (BY, NZ)
    count = 16 * len(CHUNKS) + 8
    scratch = [
        pltpu.VMEM(padded, F32), pltpu.VMEM(padded, F32),
        pltpu.VMEM(field, F32), pltpu.VMEM(field, F32), pltpu.VMEM(field, F32),
        pltpu.VMEM((2,) + field, BF16),
        pltpu.VMEM((768, 256), BF16), pltpu.VMEM((256, 768), BF16),
        pltpu.VMEM((2, NZ, 3 * NR), BF16),
        per_chunk(lambda n, h, r: (n, NY, NZ)),
        per_chunk(lambda n, h, r: (NB, r) + block),
        per_chunk(lambda n, h, r: (h, NY, NZ)),
        per_chunk(lambda n, h, r: (5, n) + block),
        per_chunk(lambda n, h, r: (5, h) + block),
        per_chunk(lambda n, h, r: (8, r) + block),
        per_chunk(lambda n, h, r: (8, r) + block),
        per_chunk(lambda n, h, r: (8, r) + block),
        per_chunk(lambda n, h, r: (3, 2, r) + block),
        per_chunk(lambda n, h, r: (r,) + block),
        per_chunk(lambda n, h, r: (n,) + block),
        pltpu.SemaphoreType.DMA((count,)),
        pltpu.SemaphoreType.DMA((count,)),
        pltpu.SemaphoreType.DMA((8 * len(CHUNKS),)),
    ]
    return pl.pallas_call(
        kernel,
        out_shape=(
            jax.ShapeDtypeStruct(field_now.shape, F32),
            jax.ShapeDtypeStruct(field_now.shape, F32),
            jax.ShapeDtypeStruct(courant.shape, F32),
        ),
        in_specs=[anywhere, anywhere, anywhere, vector, vector, anywhere, scalar, scalar],
        out_specs=(anywhere, anywhere, anywhere),
        scratch_shapes=scratch,
        compiler_params=pltpu.CompilerParams(
            collective_id=0, has_side_effects=True, vmem_limit_bytes=60 << 20),
    )(field_before, field_now, snapshots, traces, receivers, courant, aperture, block_of)


def solution(mesh):
    in_specs = (
        P("shot", "sub", None, None),
        P("shot", "sub", None, None),
        P("shot", None, "sub", None, None),
        P("shot", "sub", None, None),
        P("shot", "sub", None),
        P("sub", "shot", None),
        P(),
        P(),
    )
    out_specs = (P("shot", "sub", None, None), P("shot", "sub", None, None), P("sub", "shot", None))
    return jax.shard_map(local, mesh=mesh, in_specs=in_specs, out_specs=out_specs, check_vma=False)
```

```python
import functools

import jax
import jax.numpy as jnp
import ml_dtypes
import numpy as np
from jax import lax
from jax.experimental import pallas as pl
from jax.experimental.pallas import tpu as pltpu
from jax.sharding import PartitionSpec as P

MESH = pl.DeviceIdType.MESH
F32 = jnp.float32
BF16 = jnp.bfloat16

NX, NY, NZ, BY, NB, NR = 32, 64, 256, 16, 16, 128
HALO = 4
centre_weight = -205.0 / 72.0
side_weights = (8.0 / 5.0, -1.0 / 5.0, 8.0 / 315.0, -1.0 / 560.0)

CHUNKS = ((0, 4, 1), (4, 4, 2), (8, 4, 2), (12, 4, 2), (16, 4, 2), (20, 4, 1), (24, 4, 0), (28, 4, 0))
ORDER = (0, 7, 1, 2, 3, 4, 5, 6)
LOADS = tuple(range(1, len(CHUNKS) - 1)) + (0, len(CHUNKS) - 1)
SEQUENCE = (
    "o4", "o1", "o0", "o2", "x0", "o7", "x7", "M0", "P4", "x1", "x4", "b0", "a0", "o5",
    "x5", "b1", "P6", "a7", "a4", "P5", "P2", "x2", "b7", "a1", "o6", "x6", "d0", "b4",
    "a5", "d7", "s0", "d4", "P7", "o3", "x3", "s4", "d1", "P0", "a2", "b5", "b2", "s7",
    "17", "b6", "10", "H0", "P1", "s1", "a6", "d5", "a3", "b3", "s5", "d2", "s2", "d6",
    "P3", "d3", "14", "s3", "s6", "16", "15", "26", "p6", "11", "20", "27", "p7", "25",
    "12", "q6", "13", "23", "q7", "24", "r6", "p0", "22", "p5", "21", "q0", "q5", "p3",
    "q3", "t6", "p4", "r0", "r7", "r5", "p2", "r3", "q4", "R5", "q2", "p1", "q1", "t3",
    "t0", "t7", "r2", "R3", "r4", "t5", "R0", "r1", "R1", "R6", "t2", "R7", "R2", "t4",
    "R4", "t1", "f3", "f5", "f7", "f0", "f6", "f4", "f2", "f1",
)
OWN, A, B, D = range(4)


def split(value):
    high = value.astype(BF16)
    low = (value - high.astype(F32)).astype(BF16)
    return high, low


def band(i, j):
    apart = jnp.abs(i - j)
    high = jnp.zeros(apart.shape, F32)
    low = jnp.zeros(apart.shape, F32)
    for distance in range(1, 5):
        weight = np.float32(side_weights[distance - 1])
        top = np.float32(weight.astype(ml_dtypes.bfloat16))
        high = jnp.where(apart == distance, float(top), high)
        low = jnp.where(apart == distance, float(weight - top), low)
    return high.astype(BF16), low.astype(BF16)


def kernel(before, now, snapshots, traces, receivers, courant, aperture, block_of,
           prior_out, final_out, image_out,
           fpad, npad, base, lap, last, snap, wz, wy, spots,
           speed, gath, stage, img, imgin, sibout, sibin, acc, xin, yin, imgout,
           send_sems, recv_sems, local_sems):
    s = lax.axis_index("shot")
    u = lax.axis_index("sub")
    c = lax.rem(s, 2)
    y = lax.rem(s // 2, 2)
    x = s // 4
    way = 1 - 2 * c

    def at(x_, y_, c_):
        return {"shot": (x_ * 2 + y_) * 2 + c_, "sub": u}

    def column(role, way_):
        return lax.rem({OWN: x, A: x - way_ + 4, B: x + way_ + 4, D: x + 2}[role], 4)

    dev = {
        "A": at(column(A, way), y, c),
        "B": at(column(B, way), y, c),
        "Y": at(x, 1 - y, c),
        "C": at(x, y, 1 - c),
        "S+": {"shot": s, "sub": lax.rem(u + 1, 16)},
        "S-": {"shot": s, "sub": lax.rem(u + 15, 16)},
    }
    barrier = pltpu.get_barrier_semaphore()
    for name in dev:
        pl.semaphore_signal(barrier, inc=1, device_id=dev[name], device_id_type=MESH)
    first_two = [int(name[1:]) for name in SEQUENCE if name[0] == "2"][0]
    ids = {}
    sent = []

    def number(name):
        return ids.setdefault(name, len(ids))

    def copy_of(name, src, dst, to):
        n = number(name)
        return pltpu.make_async_remote_copy(
            src_ref=src, dst_ref=dst, send_sem=send_sems.at[n], recv_sem=recv_sems.at[n],
            device_id=dev[to], device_id_type=MESH)

    def send(name, src, dst, to):
        copy = copy_of(name, src, dst, to)
        copy.start()
        sent.append(copy)

    def arrive(name, dst):
        copy_of(name, dst, dst, "Y").wait_recv()

    locals_ = {}

    def local(name, src, dst):
        copy = pltpu.make_async_copy(src, dst, local_sems.at[len(locals_)])
        locals_[name] = copy
        copy.start()

    def shape_of(k):
        first, size, h = CHUNKS[k]
        return first, size, h, size - h

    for k in ORDER:
        first, size, h, r = shape_of(k)
        local(("own", k), courant.at[pl.ds(first + y * h, r)], gath[k].at[c * 8 + x * 2 + y])
    for k in LOADS:
        first, size, h, r = shape_of(k)
        local(("now", k), now.at[0, pl.ds(first, size)], fpad.at[pl.ds(HALO + first, size)])
    for k in LOADS:
        first, size, h, r = shape_of(k)
        local(("before", k), before.at[0, pl.ds(first, size)], base.at[pl.ds(first, size)])
    local("snap", snapshots.at[0], snap)

    pl.semaphore_wait(barrier, len(dev))

    def halo_send(name, up_src, down_src, pad):
        up = copy_of(name + "up", up_src, pad.at[pl.ds(0, HALO)], "S+")
        down = copy_of(name + "down", down_src, pad.at[pl.ds(HALO + NX, HALO)], "S-")

        @pl.when(u < 15)
        def _():
            up.start()

        @pl.when(u > 0)
        def _():
            down.start()

        return up, down

    def halo_low(copies):
        @pl.when(u > 0)
        def _():
            copies[0].wait_recv()

    def halo_high(copies):
        @pl.when(u < 15)
        def _():
            copies[1].wait_recv()

    def halo_sent(copies):
        @pl.when(u < 15)
        def _():
            copies[0].wait_send()

        @pl.when(u > 0)
        def _():
            copies[1].wait_send()

    def pair(role, c_):
        return pl.ds(c_ * 8 + 2 * column(role, 1 - 2 * c_), 2)

    def gather_y(k):
        first, size, h, r = shape_of(k)
        send(("gy", k), courant.at[pl.ds(first + (1 - y) * h, r)], gath[k].at[c * 8 + x * 2 + y], "Y")

    def gather_own(k):
        locals_[("own", k)].wait()
        mine = gath[k].at[c * 8 + x * 2 + y]
        send(("ga", 0, k), mine, mine, "A")
        send(("gb", 0, k), mine, mine, "B")

    def gather_x(k):
        theirs = gath[k].at[c * 8 + x * 2 + 1 - y]
        arrive(("gy", k), theirs)
        send(("ga", 1, k), theirs, theirs, "A")
        send(("gb", 1, k), theirs, theirs, "B")
        both = gath[k].at[pair(OWN, c)]
        send(("gc", OWN, k), both, both, "C")

    def gather_a(k):
        column_a = column(A, way)
        arrive(("gb", 0, k), gath[k].at[c * 8 + 2 * column_a + y])
        arrive(("gb", 1, k), gath[k].at[c * 8 + 2 * column_a + 1 - y])
        both = gath[k].at[pair(A, c)]
        send(("gd", k), both, both, "B")
        send(("gc", A, k), both, both, "C")

    def gather_b(k):
        column_b = column(B, way)
        arrive(("ga", 0, k), gath[k].at[c * 8 + 2 * column_b + y])
        arrive(("ga", 1, k), gath[k].at[c * 8 + 2 * column_b + 1 - y])
        both = gath[k].at[pair(B, c)]
        send(("gc", B, k), both, both, "C")

    def gather_d(k):
        both = gath[k].at[pair(D, c)]
        arrive(("gd", k), both)
        send(("gc", D, k), both, both, "C")

    def slots_from(first_block):
        found = []
        for j in range(4):
            slot = 0
            for b in range(NB):
                slot = jnp.where(block_of[b] == first_block + j, (b % 2) * 8 + b // 2, slot)
            found.append(slot)
        return found

    def gather_stage(k):
        first, size, h, r = shape_of(k)
        for role in (OWN, A, B, D):
            arrive(("gc", role, k), gath[k].at[pair(role, 1 - c)])
        for j in range(4 if h else 0):
            stage[k][:, BY * j:BY * j + BY, :] = gath[k][their_slots[j], pl.ds(y * (r - h), h)]
        if h:
            send(("gs", k), stage[k], speed[k].at[pl.ds(y * r, h)], "Y")
        for j in range(4):
            speed[k][pl.ds(y * h, r), BY * j:BY * j + BY, :] = gath[k][my_slots[j]]

    def matrices():
        i = lax.broadcasted_iota(jnp.int32, (256, 256), 0)
        j = lax.broadcasted_iota(jnp.int32, (256, 256), 1)
        high, low = band(i, j)
        wz[0:256, :] = high
        wz[256:512, :] = high
        wz[512:768, :] = low
        same = (i // NY) == (j // NY)
        high = jnp.where(same, high.astype(F32), 0.0).astype(BF16)
        low = jnp.where(same, low.astype(F32), 0.0).astype(BF16)
        wy[:, 0:256] = high
        wy[:, 256:512] = high
        wy[:, 512:768] = low

    def depth_spots():
        z = lax.broadcasted_iota(jnp.int32, (NZ, NR), 0)
        at_depth = z == lax.rem(receivers[0], NZ)
        for t in range(2):
            value = jnp.where(at_depth, traces[0, 0, t:t + 1, :], 0.0)
            high = value.astype(BF16)
            rest = value - high.astype(F32)
            middle = rest.astype(BF16)
            low = (rest - middle.astype(F32)).astype(BF16)
            spots[t, :, 0:NR] = high
            spots[t, :, NR:2 * NR] = middle
            spots[t, :, 2 * NR:3 * NR] = low

    def injected(layer, t):
        row = lax.broadcasted_iota(jnp.int32, (4 * NY, NR), 0) + layer * NY
        hit = jnp.where(row == receivers[0] // NZ, 1.0, 0.0).astype(BF16)
        hits = jnp.concatenate([hit, hit, hit], axis=1)
        return lax.dot_general(hits, spots[t], (((1,), (1,)), ((), ())), preferred_element_type=F32)

    def laplace(pad, layer):
        field = pad[pl.ds(layer + HALO, 4)]
        rows = field.reshape(4 * NY, NZ)
        high, low = split(rows)
        summed = jnp.dot(jnp.concatenate([high, low, high], axis=1), wz[...], preferred_element_type=F32)
        summed = summed + jnp.dot(wy[...], jnp.concatenate([high, low, high], axis=0), preferred_element_type=F32)
        summed = summed.reshape(4, NY, NZ) + (3.0 * centre_weight) * field
        for distance in range(1, 5):
            summed = summed + side_weights[distance - 1] * (
                pad[pl.ds(layer + HALO + distance, 4)] + pad[pl.ds(layer + HALO - distance, 4)])
        return field, summed

    def groups(k, body):
        first, size, h, r = shape_of(k)

        if size == 4:
            body(first, 0)
            return

        def step(g, carry):
            body(first + 4 * g, 4 * g)
            return carry

        lax.fori_loop(0, size // 4, step, 0)

    def prepare(k):
        if k == 0:
            halo_low(first_halo)
        if k == len(CHUNKS) - 1:
            halo_high(first_halo)
        locals_[("before", k)].wait()

        def body(layer, inside):
            field, summed = laplace(fpad, layer)
            lap[pl.ds(layer, 4)] = summed
            base[pl.ds(layer, 4)] = (2.0 * field - base[pl.ds(layer, 4)]
                                     + injected(layer, 0).reshape(4, NY, NZ))

        groups(k, body)

    def gather_end(k):
        first, size, h, r = shape_of(k)
        if h:
            arrive(("gs", k), speed[k].at[pl.ds((1 - y) * r, h)])

    def step_one(k):
        first, size, h, r = shape_of(k)
        gather_end(k)

        def body(layer, inside):
            npad[pl.ds(layer + HALO, 4)] = (base[pl.ds(layer, 4)]
                                            + speed[k][pl.ds(inside, 4)] * lap[pl.ds(layer, 4)])

        groups(k, body)
        local(("prior", k), npad.at[pl.ds(HALO + first, size)], prior_out.at[0, pl.ds(first, size)])

    def step_two(k):
        first, size, h, r = shape_of(k)
        if k == 0:
            halo_low(second_halo)
        if k == len(CHUNKS) - 1:
            halo_high(second_halo)
        if k == first_two:
            locals_["snap"].wait()

        def body(layer, inside):
            field, summed = laplace(npad, layer)
            value = (2.0 * field - fpad[pl.ds(layer + HALO, 4)] + speed[k][pl.ds(inside, 4)] * summed
                     + injected(layer, 1).reshape(4, NY, NZ))
            last[pl.ds(layer, 4)] = value
            seen = snap[0, pl.ds(layer, 4)].astype(F32) * field + snap[1, pl.ds(layer, 4)].astype(F32) * value
            for j in range(4):
                img[k][j, pl.ds(inside, 4)] = seen[:, BY * j:BY * j + BY, :]

        groups(k, body)
        local(("final", k), last.at[pl.ds(first, size)], final_out.at[0, pl.ds(first, size)])
        img[k][4] = jnp.zeros((size, BY, NZ), F32)
        if h:
            imgin[k][4] = jnp.zeros((h, BY, NZ), F32)
            send(("ry", k), img[k].at[pl.ds(0, 4), pl.ds((1 - y) * r, h)], imgin[k].at[pl.ds(0, 4)], "Y")

    def place(first_block, storage):
        block = block_of[storage] - first_block
        return jnp.where((block >= 0) & (block < 4), block, 4)

    def reduce_sibling(k):
        first, size, h, r = shape_of(k)
        if h:
            arrive(("ry", k), imgin[k].at[pl.ds(0, 4)])
        for to, core in ((sibout[k], 1 - c), (acc[k], c)):
            def body(slot, carry, to=to, core=core):
                storage = 2 * slot + core
                to[slot] = img[k][place(my_first, storage), pl.ds(y * h, r)]
                if h:
                    inner = pl.ds(y * (r - h), h)
                    to[slot, inner] = to[slot, inner] + imgin[k][place(their_first, storage)]
                return carry

            lax.fori_loop(0, 8, body, 0)
            if to is sibout[k]:
                send(("rc", k), sibout[k], sibin[k], "C")

    def reduce_x(k):
        arrive(("rc", k), sibin[k])

        def body(slot, carry):
            acc[k][slot] = acc[k][slot] + sibin[k][slot]
            return carry

        lax.fori_loop(0, 8, body, 0)
        for i, row in enumerate((1 - y, y)):
            send(("rd", i, k), acc[k].at[2 * column(D, way) + row], xin[k].at[i], "B")
            send(("ra", i, k), acc[k].at[2 * column(A, way) + row], xin[k].at[2 + i], "A")

    def reduce_forward(k, i, row):
        arrive(("rd", i, k), xin[k].at[i])
        to_b = 2 * column(B, way) + row
        acc[k][to_b] = acc[k][to_b] + xin[k][i]
        send(("rb", i, k), acc[k].at[to_b], xin[k].at[4 + i], "B")

    def reduce_theirs(k):
        reduce_forward(k, 0, 1 - y)

    def reduce_ours(k):
        reduce_forward(k, 1, y)

    def collected(k, i, row):
        arrive(("ra", i, k), xin[k].at[2 + i])
        arrive(("rb", i, k), xin[k].at[4 + i])
        return acc[k][2 * x + row] + xin[k][2 + i] + xin[k][4 + i]

    def reduce_y(k):
        acc[k][2 * x + 1 - y] = collected(k, 0, 1 - y)
        send(("rz", k), acc[k].at[2 * x + 1 - y], yin[k], "Y")

    def finish(k):
        first, size, h, r = shape_of(k)
        if h:
            imgout[k][...] = jnp.zeros((size, BY, NZ), F32)
        imgout[k][pl.ds(y * h, r)] = collected(k, 1, y)
        arrive(("rz", k), yin[k])
        theirs = pl.ds((1 - y) * h, r)
        imgout[k][theirs] = imgout[k][theirs] + yin[k][...]
        local(("image", k), imgout[k], image_out.at[pl.ds(first, size)])

    for k in ORDER:
        gather_y(k)
    first_halo = halo_send("h0", now.at[0, pl.ds(NX - HALO, HALO)], now.at[0, pl.ds(0, HALO)], fpad)
    second_halo = []
    my_first = aperture[s]
    their_first = aperture[(x * 2 + 1 - y) * 2 + c]
    my_slots = slots_from(my_first)
    their_slots = slots_from(their_first)

    def constants(k):
        @pl.when(u == 0)
        def _():
            fpad[0:HALO] = jnp.zeros((HALO, NY, NZ), F32)
            npad[0:HALO] = jnp.zeros((HALO, NY, NZ), F32)

        @pl.when(u == 15)
        def _():
            fpad[HALO + NX:] = jnp.zeros((HALO, NY, NZ), F32)
            npad[HALO + NX:] = jnp.zeros((HALO, NY, NZ), F32)

        matrices()
        depth_spots()
        for j in range(len(CHUNKS)):
            locals_[("now", j)].wait()

    def edges(k):
        second_halo.extend(halo_send("h1", npad.at[pl.ds(NX, HALO)], npad.at[pl.ds(HALO, HALO)], npad))

    steps = {
        "o": gather_own, "x": gather_x, "a": gather_a, "b": gather_b, "d": gather_d, "s": gather_stage,
        "M": constants, "P": prepare, "1": step_one, "H": edges, "2": step_two,
        "p": reduce_sibling, "q": reduce_x, "r": reduce_theirs, "R": reduce_ours, "t": reduce_y, "f": finish,
    }
    for name in SEQUENCE:
        steps[name[0]](int(name[1:]))

    halo_sent(first_halo)
    halo_sent(second_halo)
    for copy in sent:
        copy.wait_send()
    for name in locals_:
        if name[0] in ("prior", "final", "image"):
            locals_[name].wait()


def local(field_before, field_now, snapshots, traces, receivers, courant, aperture, block_of):
    anywhere = pl.BlockSpec(memory_space=pl.ANY)
    vector = pl.BlockSpec(memory_space=pltpu.VMEM)
    scalar = pl.BlockSpec(memory_space=pltpu.SMEM)

    def per_chunk(dims):
        return [pltpu.VMEM(dims(size, h, size - h), F32) for first, size, h in CHUNKS]

    field = (NX, NY, NZ)
    padded = (NX + 2 * HALO, NY, NZ)
    block = (BY, NZ)
    count = 24 * len(CHUNKS) + 8
    scratch = [
        pltpu.VMEM(padded, F32), pltpu.VMEM(padded, F32),
        pltpu.VMEM(field, F32), pltpu.VMEM(field, F32), pltpu.VMEM(field, F32),
        pltpu.VMEM((2,) + field, BF16),
        pltpu.VMEM((768, 256), BF16), pltpu.VMEM((256, 768), BF16),
        pltpu.VMEM((2, NZ, 3 * NR), BF16),
        per_chunk(lambda n, h, r: (n, NY, NZ)),
        per_chunk(lambda n, h, r: (NB, r) + block),
        per_chunk(lambda n, h, r: (max(h, 1), NY, NZ)),
        per_chunk(lambda n, h, r: (5, n) + block),
        per_chunk(lambda n, h, r: (5, max(h, 1)) + block),
        per_chunk(lambda n, h, r: (8, r) + block),
        per_chunk(lambda n, h, r: (8, r) + block),
        per_chunk(lambda n, h, r: (8, r) + block),
        per_chunk(lambda n, h, r: (6, r) + block),
        per_chunk(lambda n, h, r: (r,) + block),
        per_chunk(lambda n, h, r: (n,) + block),
        pltpu.SemaphoreType.DMA((count,)),
        pltpu.SemaphoreType.DMA((count,)),
        pltpu.SemaphoreType.DMA((8 * len(CHUNKS),)),
    ]
    return pl.pallas_call(
        kernel,
        out_shape=(
            jax.ShapeDtypeStruct(field_now.shape, F32),
            jax.ShapeDtypeStruct(field_now.shape, F32),
            jax.ShapeDtypeStruct(courant.shape, F32),
        ),
        in_specs=[anywhere, anywhere, anywhere, vector, vector, anywhere, scalar, scalar],
        out_specs=(anywhere, anywhere, anywhere),
        scratch_shapes=scratch,
        compiler_params=pltpu.CompilerParams(
            collective_id=0, has_side_effects=True, vmem_limit_bytes=60 << 20),
    )(field_before, field_now, snapshots, traces, receivers, courant, aperture, block_of)


def solution(mesh):
    in_specs = (
        P("shot", "sub", None, None),
        P("shot", "sub", None, None),
        P("shot", None, "sub", None, None),
        P("shot", "sub", None, None),
        P("shot", "sub", None),
        P("sub", "shot", None),
        P(),
        P(),
    )
    out_specs = (P("shot", "sub", None, None), P("shot", "sub", None, None), P("sub", "shot", None))
    return jax.shard_map(local, mesh=mesh, in_specs=in_specs, out_specs=out_specs, check_vma=False)
```

```python
import functools

import jax
import jax.numpy as jnp
import ml_dtypes
import numpy as np
from jax import lax
from jax.experimental import pallas as pl
from jax.experimental.pallas import tpu as pltpu
from jax.sharding import PartitionSpec as P

MESH = pl.DeviceIdType.MESH
F32 = jnp.float32
BF16 = jnp.bfloat16

NX, NY, NZ, BY, NB, NR = 32, 64, 256, 16, 16, 128
HALO = 4
centre_weight = -205.0 / 72.0
side_weights = (8.0 / 5.0, -1.0 / 5.0, 8.0 / 315.0, -1.0 / 560.0)

CHUNKS = ((0, 4, 1), (4, 4, 2), (8, 4, 2), (12, 4, 2), (16, 4, 2), (20, 4, 1), (24, 4, 0), (28, 4, 0))
ORDER = (0, 7, 1, 2, 3, 4, 5, 6)
LOADS = tuple(range(1, len(CHUNKS) - 1)) + (0, len(CHUNKS) - 1)
SEQUENCE = (
    "o4", "o1", "o0", "o2", "x0", "o7", "x7", "Z0", "M0", "P4", "x1", "x4", "b0", "a0",
    "o5", "x5", "b1", "P6", "a7", "a4", "P5", "P2", "x2", "b7", "a1", "o6", "x6", "d0",
    "b4", "a5", "d7", "s0", "d4", "P7", "o3", "x3", "s4", "d1", "P0", "a2", "b5", "b2",
    "s7", "17", "b6", "10", "H0", "P1", "s1", "a6", "d5", "a3", "b3", "s5", "d2", "s2",
    "d6", "P3", "d3", "14", "s3", "s6", "16", "15", "26", "p6", "11", "20", "27", "p7",
    "25", "12", "q6", "13", "23", "q7", "24", "r6", "p0", "22", "p5", "21", "q0", "q5",
    "p3", "q3", "t6", "p4", "r0", "r7", "r5", "p2", "r3", "q4", "R5", "q2", "p1", "q1",
    "t3", "t0", "t7", "r2", "R3", "r4", "t5", "R0", "r1", "R1", "R6", "t2", "R7", "R2",
    "t4", "R4", "t1", "f3", "f5", "f7", "f0", "f6", "f4", "f2", "f1",
)
OWN, A, B, D = range(4)


def split(value):
    high = value.astype(BF16)
    low = (value - high.astype(F32)).astype(BF16)
    return high, low


def band(i, j):
    apart = jnp.abs(i - j)
    high = jnp.zeros(apart.shape, F32)
    low = jnp.zeros(apart.shape, F32)
    for distance in range(1, 5):
        weight = np.float32(side_weights[distance - 1])
        top = np.float32(weight.astype(ml_dtypes.bfloat16))
        high = jnp.where(apart == distance, float(top), high)
        low = jnp.where(apart == distance, float(weight - top), low)
    return high.astype(BF16), low.astype(BF16)


def kernel(before, now, snapshots, traces_in, receivers_in, courant, aperture_in, block_of_in,
           prior_out, final_out, image_out,
           traces, receivers, aperture, block_of, fpad, npad, base, lap, last, snap, wz, wy, spots,
           speed, gath, stage, img, imgin, sibout, sibin, acc, xin, yin, imgout,
           send_sems, recv_sems, local_sems, inside, inside_sub):
    s = lax.axis_index("shot")
    u = lax.axis_index("sub")
    c = lax.rem(s, 2)
    y = lax.rem(s // 2, 2)
    x = s // 4
    way = 1 - 2 * c

    def at(x_, y_, c_):
        return {"shot": (x_ * 2 + y_) * 2 + c_, "sub": u}

    def column(role, way_):
        return lax.rem({OWN: x, A: x - way_ + 4, B: x + way_ + 4, D: x + 2}[role], 4)

    dev = {
        "A": at(column(A, way), y, c),
        "B": at(column(B, way), y, c),
        "Y": at(x, 1 - y, c),
        "C": at(x, y, 1 - c),
        "S+": {"shot": s, "sub": lax.rem(u + 1, 16)},
        "S-": {"shot": s, "sub": lax.rem(u + 15, 16)},
    }
    barrier = pltpu.get_barrier_semaphore()

    def tell(semaphore, name):
        pl.semaphore_signal(semaphore, inc=1, device_id=dev[name], device_id_type=MESH)

    @pl.when(c == 0)
    def _():
        for name in "ABY":
            tell(barrier, name)

    @pl.when(c == 1)
    def _():
        tell(barrier, "C")

    first_two = [int(name[1:]) for name in SEQUENCE if name[0] == "2"][0]
    ids = {}
    sent = []

    def number(name):
        return ids.setdefault(name, len(ids))

    def copy_of(name, src, dst, to):
        n = number(name)
        return pltpu.make_async_remote_copy(
            src_ref=src, dst_ref=dst, send_sem=send_sems.at[n], recv_sem=recv_sems.at[n],
            device_id=dev[to], device_id_type=MESH)

    def send(name, src, dst, to):
        copy = copy_of(name, src, dst, to)
        copy.start()
        sent.append(copy)

    def arrive(name, dst):
        copy_of(name, dst, dst, "Y").wait_recv()

    locals_ = {}

    def local(name, src, dst):
        copy = pltpu.make_async_copy(src, dst, local_sems.at[len(locals_)])
        locals_[name] = copy
        copy.start()

    def shape_of(k):
        first, size, h = CHUNKS[k]
        return first, size, h, size - h

    for k in ORDER:
        first, size, h, r = shape_of(k)
        local(("own", k), courant.at[pl.ds(first + y * h, r)], gath[k].at[c * 8 + x * 2 + y])
    for k in LOADS:
        first, size, h, r = shape_of(k)
        local(("now", k), now.at[0, pl.ds(first, size)], fpad.at[pl.ds(HALO + first, size)])
    for k in LOADS:
        first, size, h, r = shape_of(k)
        local(("before", k), before.at[0, pl.ds(first, size)], base.at[pl.ds(first, size)])
    local("snap", snapshots.at[0], snap)
    for name, src, dst in (("traces", traces_in, traces), ("receivers", receivers_in, receivers),
                           ("aperture", aperture_in, aperture), ("block_of", block_of_in, block_of)):
        local(name, src, dst)

    @pl.when(c == 0)
    def _():
        pl.semaphore_wait(barrier, 4)
        for name in "ABY":
            tell(inside, name)
        pl.semaphore_wait(inside, 3)
        tell(inside, "C")

    @pl.when(c == 1)
    def _():
        pl.semaphore_wait(inside, 1)
        tell(barrier, "S+")
        tell(barrier, "S-")


    def halo_send(name, up_src, down_src, pad):
        up = copy_of(name + "up", up_src, pad.at[pl.ds(0, HALO)], "S+")
        down = copy_of(name + "down", down_src, pad.at[pl.ds(HALO + NX, HALO)], "S-")

        @pl.when(u < 15)
        def _():
            up.start()

        @pl.when(u > 0)
        def _():
            down.start()

        return up, down

    def halo_low(copies):
        @pl.when(u > 0)
        def _():
            copies[0].wait_recv()

    def halo_high(copies):
        @pl.when(u < 15)
        def _():
            copies[1].wait_recv()

    def halo_sent(copies):
        @pl.when(u < 15)
        def _():
            copies[0].wait_send()

        @pl.when(u > 0)
        def _():
            copies[1].wait_send()

    def pair(role, c_):
        return pl.ds(c_ * 8 + 2 * column(role, 1 - 2 * c_), 2)

    def gather_y(k):
        first, size, h, r = shape_of(k)
        send(("gy", k), courant.at[pl.ds(first + (1 - y) * h, r)], gath[k].at[c * 8 + x * 2 + y], "Y")

    def gather_own(k):
        locals_[("own", k)].wait()
        mine = gath[k].at[c * 8 + x * 2 + y]
        send(("ga", 0, k), mine, mine, "A")
        send(("gb", 0, k), mine, mine, "B")

    def gather_x(k):
        theirs = gath[k].at[c * 8 + x * 2 + 1 - y]
        arrive(("gy", k), theirs)
        send(("ga", 1, k), theirs, theirs, "A")
        send(("gb", 1, k), theirs, theirs, "B")
        both = gath[k].at[pair(OWN, c)]
        send(("gc", OWN, k), both, both, "C")

    def gather_a(k):
        column_a = column(A, way)
        arrive(("gb", 0, k), gath[k].at[c * 8 + 2 * column_a + y])
        arrive(("gb", 1, k), gath[k].at[c * 8 + 2 * column_a + 1 - y])
        both = gath[k].at[pair(A, c)]
        send(("gd", k), both, both, "B")
        send(("gc", A, k), both, both, "C")

    def gather_b(k):
        column_b = column(B, way)
        arrive(("ga", 0, k), gath[k].at[c * 8 + 2 * column_b + y])
        arrive(("ga", 1, k), gath[k].at[c * 8 + 2 * column_b + 1 - y])
        both = gath[k].at[pair(B, c)]
        send(("gc", B, k), both, both, "C")

    def gather_d(k):
        both = gath[k].at[pair(D, c)]
        arrive(("gd", k), both)
        send(("gc", D, k), both, both, "C")

    def slots_from(first_block):
        found = []
        for j in range(4):
            slot = 0
            for b in range(NB):
                slot = jnp.where(block_of[b] == first_block + j, (b % 2) * 8 + b // 2, slot)
            found.append(slot)
        return found

    def gather_stage(k):
        first, size, h, r = shape_of(k)
        for role in (OWN, A, B, D):
            arrive(("gc", role, k), gath[k].at[pair(role, 1 - c)])
        for j in range(4 if h else 0):
            stage[k][:, BY * j:BY * j + BY, :] = gath[k][their_slots[j], pl.ds(y * (r - h), h)]
        if h:
            send(("gs", k), stage[k], speed[k].at[pl.ds(y * r, h)], "Y")
        for j in range(4):
            speed[k][pl.ds(y * h, r), BY * j:BY * j + BY, :] = gath[k][my_slots[j]]

    def matrices():
        i = lax.broadcasted_iota(jnp.int32, (256, 256), 0)
        j = lax.broadcasted_iota(jnp.int32, (256, 256), 1)
        high, low = band(i, j)
        wz[0:256, :] = high
        wz[256:512, :] = high
        wz[512:768, :] = low
        same = (i // NY) == (j // NY)
        high = jnp.where(same, high.astype(F32), 0.0).astype(BF16)
        low = jnp.where(same, low.astype(F32), 0.0).astype(BF16)
        wy[:, 0:256] = high
        wy[:, 256:512] = high
        wy[:, 512:768] = low

    def depth_spots():
        z = lax.broadcasted_iota(jnp.int32, (NZ, NR), 0)
        at_depth = z == lax.rem(receivers[0], NZ)
        for t in range(2):
            value = jnp.where(at_depth, traces[0, 0, t:t + 1, :], 0.0)
            high = value.astype(BF16)
            rest = value - high.astype(F32)
            middle = rest.astype(BF16)
            low = (rest - middle.astype(F32)).astype(BF16)
            spots[t, :, 0:NR] = high
            spots[t, :, NR:2 * NR] = middle
            spots[t, :, 2 * NR:3 * NR] = low

    def injected(layer, t):
        row = lax.broadcasted_iota(jnp.int32, (4 * NY, NR), 0) + layer * NY
        hit = jnp.where(row == receivers[0] // NZ, 1.0, 0.0).astype(BF16)
        hits = jnp.concatenate([hit, hit, hit], axis=1)
        return lax.dot_general(hits, spots[t], (((1,), (1,)), ((), ())), preferred_element_type=F32)

    def laplace(pad, layer):
        field = pad[pl.ds(layer + HALO, 4)]
        rows = field.reshape(4 * NY, NZ)
        high, low = split(rows)
        summed = jnp.dot(jnp.concatenate([high, low, high], axis=1), wz[...], preferred_element_type=F32)
        summed = summed + jnp.dot(wy[...], jnp.concatenate([high, low, high], axis=0), preferred_element_type=F32)
        summed = summed.reshape(4, NY, NZ) + (3.0 * centre_weight) * field
        for distance in range(1, 5):
            summed = summed + side_weights[distance - 1] * (
                pad[pl.ds(layer + HALO + distance, 4)] + pad[pl.ds(layer + HALO - distance, 4)])
        return field, summed

    def groups(k, body):
        first, size, h, r = shape_of(k)

        if size == 4:
            body(first, 0)
            return

        def step(g, carry):
            body(first + 4 * g, 4 * g)
            return carry

        lax.fori_loop(0, size // 4, step, 0)

    def prepare(k):
        if k == 0:
            halo_low(first_halo)
        if k == len(CHUNKS) - 1:
            halo_high(first_halo)
        locals_[("before", k)].wait()

        def body(layer, inside):
            field, summed = laplace(fpad, layer)
            lap[pl.ds(layer, 4)] = summed
            base[pl.ds(layer, 4)] = (2.0 * field - base[pl.ds(layer, 4)]
                                     + injected(layer, 0).reshape(4, NY, NZ))

        groups(k, body)

    def gather_end(k):
        first, size, h, r = shape_of(k)
        if h:
            arrive(("gs", k), speed[k].at[pl.ds((1 - y) * r, h)])

    def step_one(k):
        first, size, h, r = shape_of(k)
        gather_end(k)

        def body(layer, inside):
            npad[pl.ds(layer + HALO, 4)] = (base[pl.ds(layer, 4)]
                                            + speed[k][pl.ds(inside, 4)] * lap[pl.ds(layer, 4)])

        groups(k, body)
        local(("prior", k), npad.at[pl.ds(HALO + first, size)], prior_out.at[0, pl.ds(first, size)])

    def step_two(k):
        first, size, h, r = shape_of(k)
        if k == 0:
            halo_low(second_halo)
        if k == len(CHUNKS) - 1:
            halo_high(second_halo)
        if k == first_two:
            locals_["snap"].wait()

        def body(layer, inside):
            field, summed = laplace(npad, layer)
            value = (2.0 * field - fpad[pl.ds(layer + HALO, 4)] + speed[k][pl.ds(inside, 4)] * summed
                     + injected(layer, 1).reshape(4, NY, NZ))
            last[pl.ds(layer, 4)] = value
            seen = snap[0, pl.ds(layer, 4)].astype(F32) * field + snap[1, pl.ds(layer, 4)].astype(F32) * value
            for j in range(4):
                img[k][j, pl.ds(inside, 4)] = seen[:, BY * j:BY * j + BY, :]

        groups(k, body)
        local(("final", k), last.at[pl.ds(first, size)], final_out.at[0, pl.ds(first, size)])
        img[k][4] = jnp.zeros((size, BY, NZ), F32)
        if h:
            imgin[k][4] = jnp.zeros((h, BY, NZ), F32)
            send(("ry", k), img[k].at[pl.ds(0, 4), pl.ds((1 - y) * r, h)], imgin[k].at[pl.ds(0, 4)], "Y")

    def place(first_block, storage):
        block = block_of[storage] - first_block
        return jnp.where((block >= 0) & (block < 4), block, 4)

    def reduce_sibling(k):
        first, size, h, r = shape_of(k)
        if h:
            arrive(("ry", k), imgin[k].at[pl.ds(0, 4)])
        for to, core in ((sibout[k], 1 - c), (acc[k], c)):
            def body(slot, carry, to=to, core=core):
                storage = 2 * slot + core
                to[slot] = img[k][place(my_first, storage), pl.ds(y * h, r)]
                if h:
                    inner = pl.ds(y * (r - h), h)
                    to[slot, inner] = to[slot, inner] + imgin[k][place(their_first, storage)]
                return carry

            lax.fori_loop(0, 8, body, 0)
            if to is sibout[k]:
                send(("rc", k), sibout[k], sibin[k], "C")

    def reduce_x(k):
        arrive(("rc", k), sibin[k])

        def body(slot, carry):
            acc[k][slot] = acc[k][slot] + sibin[k][slot]
            return carry

        lax.fori_loop(0, 8, body, 0)
        for i, row in enumerate((1 - y, y)):
            send(("rd", i, k), acc[k].at[2 * column(D, way) + row], xin[k].at[i], "B")
            send(("ra", i, k), acc[k].at[2 * column(A, way) + row], xin[k].at[2 + i], "A")

    def reduce_forward(k, i, row):
        arrive(("rd", i, k), xin[k].at[i])
        to_b = 2 * column(B, way) + row
        acc[k][to_b] = acc[k][to_b] + xin[k][i]
        send(("rb", i, k), acc[k].at[to_b], xin[k].at[4 + i], "B")

    def reduce_theirs(k):
        reduce_forward(k, 0, 1 - y)

    def reduce_ours(k):
        reduce_forward(k, 1, y)

    def collected(k, i, row):
        arrive(("ra", i, k), xin[k].at[2 + i])
        arrive(("rb", i, k), xin[k].at[4 + i])
        return acc[k][2 * x + row] + xin[k][2 + i] + xin[k][4 + i]

    def reduce_y(k):
        acc[k][2 * x + 1 - y] = collected(k, 0, 1 - y)
        send(("rz", k), acc[k].at[2 * x + 1 - y], yin[k], "Y")

    def finish(k):
        first, size, h, r = shape_of(k)
        if h:
            imgout[k][...] = jnp.zeros((size, BY, NZ), F32)
        imgout[k][pl.ds(y * h, r)] = collected(k, 1, y)
        arrive(("rz", k), yin[k])
        theirs = pl.ds((1 - y) * h, r)
        imgout[k][theirs] = imgout[k][theirs] + yin[k][...]
        local(("image", k), imgout[k], image_out.at[pl.ds(first, size)])

    for k in ORDER:
        gather_y(k)
    first_halo = []
    second_halo = []

    def first_edges(k):
        @pl.when(c == 1)
        def _():
            pl.semaphore_wait(barrier, 2)
            tell(inside_sub, "C")

        @pl.when(c == 0)
        def _():
            pl.semaphore_wait(inside_sub, 1)

        first_halo.extend(halo_send("h0", now.at[0, pl.ds(NX - HALO, HALO)], now.at[0, pl.ds(0, HALO)], fpad))

    for name in ("traces", "receivers", "aperture", "block_of"):
        locals_[name].wait()
    my_first = aperture[s]
    their_first = aperture[(x * 2 + 1 - y) * 2 + c]
    my_slots = slots_from(my_first)
    their_slots = slots_from(their_first)

    def constants(k):
        @pl.when(u == 0)
        def _():
            fpad[0:HALO] = jnp.zeros((HALO, NY, NZ), F32)
            npad[0:HALO] = jnp.zeros((HALO, NY, NZ), F32)

        @pl.when(u == 15)
        def _():
            fpad[HALO + NX:] = jnp.zeros((HALO, NY, NZ), F32)
            npad[HALO + NX:] = jnp.zeros((HALO, NY, NZ), F32)

        matrices()
        depth_spots()
        for j in range(len(CHUNKS)):
            locals_[("now", j)].wait()

    def edges(k):
        second_halo.extend(halo_send("h1", npad.at[pl.ds(NX, HALO)], npad.at[pl.ds(HALO, HALO)], npad))

    steps = {
        "o": gather_own, "x": gather_x, "a": gather_a, "b": gather_b, "d": gather_d, "s": gather_stage,
        "Z": first_edges, "M": constants, "P": prepare, "1": step_one, "H": edges, "2": step_two,
        "p": reduce_sibling, "q": reduce_x, "r": reduce_theirs, "R": reduce_ours, "t": reduce_y, "f": finish,
    }
    for name in SEQUENCE:
        steps[name[0]](int(name[1:]))

    halo_sent(first_halo)
    halo_sent(second_halo)
    for copy in sent:
        copy.wait_send()
    for name in locals_:
        if name[0] in ("prior", "final", "image"):
            locals_[name].wait()


def local(field_before, field_now, snapshots, traces, receivers, courant, aperture, block_of):
    anywhere = pl.BlockSpec(memory_space=pl.ANY)

    def per_chunk(dims):
        return [pltpu.VMEM(dims(size, h, size - h), F32) for first, size, h in CHUNKS]

    field = (NX, NY, NZ)
    padded = (NX + 2 * HALO, NY, NZ)
    block = (BY, NZ)
    count = 24 * len(CHUNKS) + 8
    scratch = [
        pltpu.VMEM(traces.shape, F32), pltpu.VMEM(receivers.shape, jnp.int32),
        pltpu.SMEM(aperture.shape, jnp.int32), pltpu.SMEM(block_of.shape, jnp.int32),
        pltpu.VMEM(padded, F32), pltpu.VMEM(padded, F32),
        pltpu.VMEM(field, F32), pltpu.VMEM(field, F32), pltpu.VMEM(field, F32),
        pltpu.VMEM((2,) + field, BF16),
        pltpu.VMEM((768, 256), BF16), pltpu.VMEM((256, 768), BF16),
        pltpu.VMEM((2, NZ, 3 * NR), BF16),
        per_chunk(lambda n, h, r: (n, NY, NZ)),
        per_chunk(lambda n, h, r: (NB, r) + block),
        per_chunk(lambda n, h, r: (max(h, 1), NY, NZ)),
        per_chunk(lambda n, h, r: (5, n) + block),
        per_chunk(lambda n, h, r: (5, max(h, 1)) + block),
        per_chunk(lambda n, h, r: (8, r) + block),
        per_chunk(lambda n, h, r: (8, r) + block),
        per_chunk(lambda n, h, r: (8, r) + block),
        per_chunk(lambda n, h, r: (6, r) + block),
        per_chunk(lambda n, h, r: (r,) + block),
        per_chunk(lambda n, h, r: (n,) + block),
        pltpu.SemaphoreType.DMA((count,)),
        pltpu.SemaphoreType.DMA((count,)),
        pltpu.SemaphoreType.DMA((8 * len(CHUNKS),)),
        pltpu.SemaphoreType.REGULAR,
        pltpu.SemaphoreType.REGULAR,
    ]
    return pl.pallas_call(
        kernel,
        out_shape=(
            jax.ShapeDtypeStruct(field_now.shape, F32),
            jax.ShapeDtypeStruct(field_now.shape, F32),
            jax.ShapeDtypeStruct(courant.shape, F32),
        ),
        in_specs=[pl.BlockSpec(memory_space=pltpu.HBM)] * 8,
        out_specs=(anywhere, anywhere, anywhere),
        scratch_shapes=scratch,
        compiler_params=pltpu.CompilerParams(
            collective_id=0, has_side_effects=True, vmem_limit_bytes=60 << 20),
    )(field_before, field_now, snapshots, traces, receivers, courant, aperture, block_of)


def solution(mesh):
    in_specs = (
        P("shot", "sub", None, None),
        P("shot", "sub", None, None),
        P("shot", None, "sub", None, None),
        P("shot", "sub", None, None),
        P("shot", "sub", None),
        P("sub", "shot", None),
        P(),
        P(),
    )
    out_specs = (P("shot", "sub", None, None), P("shot", "sub", None, None), P("sub", "shot", None))
    return jax.shard_map(local, mesh=mesh, in_specs=in_specs, out_specs=out_specs, check_vma=False)
```

```python
import functools

import jax
import jax.numpy as jnp
import ml_dtypes
import numpy as np
from jax import lax
from jax.experimental import pallas as pl
from jax.experimental.pallas import tpu as pltpu
from jax.sharding import PartitionSpec as P

MESH = pl.DeviceIdType.MESH
F32 = jnp.float32
BF16 = jnp.bfloat16

NX, NY, NZ, BY, NB, NR = 32, 64, 256, 16, 16, 128
HALO = 4
centre_weight = -205.0 / 72.0
side_weights = (8.0 / 5.0, -1.0 / 5.0, 8.0 / 315.0, -1.0 / 560.0)

CHUNKS = ((0, 4, 2), (4, 4, 0), (8, 4, 2), (12, 4, 0), (16, 4, 1), (20, 4, 2), (24, 4, 2), (28, 4, 0))
ORDER = (7, 0, 1, 2, 3, 4, 5, 6)
LOADS = tuple(range(1, len(CHUNKS) - 1)) + (0, len(CHUNKS) - 1)
SEQUENCE = (
    "o7", "o0", "M0", "o5", "o2", "x0", "x7", "Z0", "x2", "o1", "a0", "P4", "a7", "b0",
    "a2", "P2", "o4", "x4", "b2", "d0", "o3", "s0", "o6", "x6", "x5", "d2", "b7", "x1",
    "s2", "d7", "P0", "P7", "a4", "x3", "s7", "17", "10", "H0", "a6", "b6", "P3", "b1",
    "b4", "a1", "d4", "b5", "a5", "a3", "12", "s4", "d6", "d1", "s6", "d5", "b3", "P1",
    "s1", "d3", "11", "s5", "21", "p1", "14", "s3", "13", "23", "p3", "22", "P6", "q1",
    "P5", "16", "27", "q3", "p7", "15", "26", "24", "r1", "20", "25", "r3", "q7", "p2",
    "q2", "p6", "r7", "p4", "q6", "p0", "t3", "r2", "q4", "q0", "p5", "t7", "t1", "r4",
    "q5", "r0", "t2", "r6", "R3", "r5", "R0", "t4", "R4", "R1", "R6", "t0", "t6", "R2",
    "R7", "t5", "R5", "f1", "f3", "f2", "f6", "f4", "f0", "f7", "f5",
)
OWN, A, B, D = range(4)


def split(value):
    high = value.astype(BF16)
    low = (value - high.astype(F32)).astype(BF16)
    return high, low


def band(i, j):
    apart = jnp.abs(i - j)
    high = jnp.zeros(apart.shape, F32)
    low = jnp.zeros(apart.shape, F32)
    for distance in range(1, 5):
        weight = np.float32(side_weights[distance - 1])
        top = np.float32(weight.astype(ml_dtypes.bfloat16))
        high = jnp.where(apart == distance, float(top), high)
        low = jnp.where(apart == distance, float(weight - top), low)
    return high.astype(BF16), low.astype(BF16)


def kernel(before, now, snapshots, traces_in, receivers_in, courant, aperture_in, block_of_in,
           prior_out, final_out, image_out,
           traces, receivers, aperture, block_of, fpad, npad, base, lap, last, snap, wz, wy, spots,
           speed, gath, stage, img, imgin, sibout, sibin, acc, xin, yin, imgout,
           send_sems, recv_sems, local_sems, inside, inside_sub):
    s = lax.axis_index("shot")
    u = lax.axis_index("sub")
    c = lax.rem(s, 2)
    y = lax.rem(s // 2, 2)
    x = s // 4
    way = 1 - 2 * c

    def at(x_, y_, c_):
        return {"shot": (x_ * 2 + y_) * 2 + c_, "sub": u}

    def column(role, way_):
        return lax.rem({OWN: x, A: x - way_ + 4, B: x + way_ + 4, D: x + 2}[role], 4)

    dev = {
        "A": at(column(A, way), y, c),
        "B": at(column(B, way), y, c),
        "Y": at(x, 1 - y, c),
        "C": at(x, y, 1 - c),
        "S+": {"shot": s, "sub": lax.rem(u + 1, 16)},
        "S-": {"shot": s, "sub": lax.rem(u + 15, 16)},
    }
    barrier = pltpu.get_barrier_semaphore()

    def tell(semaphore, name):
        pl.semaphore_signal(semaphore, inc=1, device_id=dev[name], device_id_type=MESH)

    @pl.when(c == 0)
    def _():
        for name in "ABY":
            tell(barrier, name)

    @pl.when(c == 1)
    def _():
        tell(barrier, "C")

    first_two = [int(name[1:]) for name in SEQUENCE if name[0] == "2"][0]
    ids = {}
    sent = []

    def number(name):
        return ids.setdefault(name, len(ids))

    def copy_of(name, src, dst, to):
        n = number(name)
        return pltpu.make_async_remote_copy(
            src_ref=src, dst_ref=dst, send_sem=send_sems.at[n], recv_sem=recv_sems.at[n],
            device_id=dev[to], device_id_type=MESH)

    def send(name, src, dst, to):
        copy = copy_of(name, src, dst, to)
        copy.start()
        sent.append(copy)

    def arrive(name, dst):
        copy_of(name, dst, dst, "Y").wait_recv()

    locals_ = {}

    def local(name, src, dst):
        copy = pltpu.make_async_copy(src, dst, local_sems.at[len(locals_)])
        locals_[name] = copy
        copy.start()

    def shape_of(k):
        first, size, h = CHUNKS[k]
        return first, size, h, size - h

    for k in ORDER:
        first, size, h, r = shape_of(k)
        local(("own", k), courant.at[pl.ds(first + y * h, r)], gath[k].at[c * 8 + x * 2 + y])
    for k in LOADS:
        first, size, h, r = shape_of(k)
        local(("now", k), now.at[0, pl.ds(first, size)], fpad.at[pl.ds(HALO + first, size)])
    for k in LOADS:
        first, size, h, r = shape_of(k)
        local(("before", k), before.at[0, pl.ds(first, size)], base.at[pl.ds(first, size)])
    local("snap", snapshots.at[0], snap)
    for name, src, dst in (("traces", traces_in, traces), ("receivers", receivers_in, receivers),
                           ("aperture", aperture_in, aperture), ("block_of", block_of_in, block_of)):
        local(name, src, dst)

    @pl.when(c == 0)
    def _():
        pl.semaphore_wait(barrier, 4)
        for name in "ABY":
            tell(inside, name)
        pl.semaphore_wait(inside, 3)
        tell(inside, "C")

    @pl.when(c == 1)
    def _():
        pl.semaphore_wait(inside, 1)
        tell(barrier, "S+")
        tell(barrier, "S-")


    def halo_send(name, up_src, down_src, pad):
        up = copy_of(name + "up", up_src, pad.at[pl.ds(0, HALO)], "S+")
        down = copy_of(name + "down", down_src, pad.at[pl.ds(HALO + NX, HALO)], "S-")

        @pl.when(u < 15)
        def _():
            up.start()

        @pl.when(u > 0)
        def _():
            down.start()

        return up, down

    def halo_low(copies):
        @pl.when(u > 0)
        def _():
            copies[0].wait_recv()

    def halo_high(copies):
        @pl.when(u < 15)
        def _():
            copies[1].wait_recv()

    def halo_sent(copies):
        @pl.when(u < 15)
        def _():
            copies[0].wait_send()

        @pl.when(u > 0)
        def _():
            copies[1].wait_send()

    def pair(role, c_):
        return pl.ds(c_ * 8 + 2 * column(role, 1 - 2 * c_), 2)

    def gather_y(k):
        first, size, h, r = shape_of(k)
        send(("gy", k), courant.at[pl.ds(first + (1 - y) * h, r)], gath[k].at[c * 8 + x * 2 + y], "Y")

    def gather_own(k):
        locals_[("own", k)].wait()
        mine = gath[k].at[c * 8 + x * 2 + y]
        send(("ga", 0, k), mine, mine, "A")
        send(("gb", 0, k), mine, mine, "B")

    def gather_x(k):
        theirs = gath[k].at[c * 8 + x * 2 + 1 - y]
        arrive(("gy", k), theirs)
        send(("ga", 1, k), theirs, theirs, "A")
        send(("gb", 1, k), theirs, theirs, "B")
        both = gath[k].at[pair(OWN, c)]
        send(("gc", OWN, k), both, both, "C")

    def gather_a(k):
        column_a = column(A, way)
        arrive(("gb", 0, k), gath[k].at[c * 8 + 2 * column_a + y])
        arrive(("gb", 1, k), gath[k].at[c * 8 + 2 * column_a + 1 - y])
        both = gath[k].at[pair(A, c)]
        send(("gd", k), both, both, "B")
        send(("gc", A, k), both, both, "C")

    def gather_b(k):
        column_b = column(B, way)
        arrive(("ga", 0, k), gath[k].at[c * 8 + 2 * column_b + y])
        arrive(("ga", 1, k), gath[k].at[c * 8 + 2 * column_b + 1 - y])
        both = gath[k].at[pair(B, c)]
        send(("gc", B, k), both, both, "C")

    def gather_d(k):
        both = gath[k].at[pair(D, c)]
        arrive(("gd", k), both)
        send(("gc", D, k), both, both, "C")

    def slots_from(first_block):
        found = []
        for j in range(4):
            slot = 0
            for b in range(NB):
                slot = jnp.where(block_of[b] == first_block + j, (b % 2) * 8 + b // 2, slot)
            found.append(slot)
        return found

    def gather_stage(k):
        first, size, h, r = shape_of(k)
        for role in (OWN, A, B, D):
            arrive(("gc", role, k), gath[k].at[pair(role, 1 - c)])
        for j in range(4 if h else 0):
            stage[k][:, BY * j:BY * j + BY, :] = gath[k][their_slots[j], pl.ds(y * (r - h), h)]
        if h:
            send(("gs", k), stage[k], speed[k].at[pl.ds(y * r, h)], "Y")
        for j in range(4):
            speed[k][pl.ds(y * h, r), BY * j:BY * j + BY, :] = gath[k][my_slots[j]]

    def matrices():
        i = lax.broadcasted_iota(jnp.int32, (256, 256), 0)
        j = lax.broadcasted_iota(jnp.int32, (256, 256), 1)
        high, low = band(i, j)
        wz[0:256, :] = high
        wz[256:512, :] = high
        wz[512:768, :] = low
        same = (i // NY) == (j // NY)
        high = jnp.where(same, high.astype(F32), 0.0).astype(BF16)
        low = jnp.where(same, low.astype(F32), 0.0).astype(BF16)
        wy[:, 0:256] = high
        wy[:, 256:512] = high
        wy[:, 512:768] = low

    def depth_spots():
        z = lax.broadcasted_iota(jnp.int32, (NZ, NR), 0)
        at_depth = z == lax.rem(receivers[0], NZ)
        for t in range(2):
            value = jnp.where(at_depth, traces[0, 0, t:t + 1, :], 0.0)
            high = value.astype(BF16)
            rest = value - high.astype(F32)
            middle = rest.astype(BF16)
            low = (rest - middle.astype(F32)).astype(BF16)
            spots[t, :, 0:NR] = high
            spots[t, :, NR:2 * NR] = middle
            spots[t, :, 2 * NR:3 * NR] = low

    def injected(layer, t):
        row = lax.broadcasted_iota(jnp.int32, (4 * NY, NR), 0) + layer * NY
        hit = jnp.where(row == receivers[0] // NZ, 1.0, 0.0).astype(BF16)
        hits = jnp.concatenate([hit, hit, hit], axis=1)
        return lax.dot_general(hits, spots[t], (((1,), (1,)), ((), ())), preferred_element_type=F32)

    def laplace(pad, layer):
        field = pad[pl.ds(layer + HALO, 4)]
        rows = field.reshape(4 * NY, NZ)
        high, low = split(rows)
        summed = jnp.dot(jnp.concatenate([high, low, high], axis=1), wz[...], preferred_element_type=F32)
        summed = summed + jnp.dot(wy[...], jnp.concatenate([high, low, high], axis=0), preferred_element_type=F32)
        summed = summed.reshape(4, NY, NZ) + (3.0 * centre_weight) * field
        for distance in range(1, 5):
            summed = summed + side_weights[distance - 1] * (
                pad[pl.ds(layer + HALO + distance, 4)] + pad[pl.ds(layer + HALO - distance, 4)])
        return field, summed

    def groups(k, body):
        first, size, h, r = shape_of(k)

        if size == 4:
            body(first, 0)
            return

        def step(g, carry):
            body(first + 4 * g, 4 * g)
            return carry

        lax.fori_loop(0, size // 4, step, 0)

    def prepare(k):
        if k == 0:
            halo_low(first_halo)
        if k == len(CHUNKS) - 1:
            halo_high(first_halo)
        locals_[("before", k)].wait()

        def body(layer, inside):
            field, summed = laplace(fpad, layer)
            lap[pl.ds(layer, 4)] = summed
            base[pl.ds(layer, 4)] = (2.0 * field - base[pl.ds(layer, 4)]
                                     + injected(layer, 0).reshape(4, NY, NZ))

        groups(k, body)

    def gather_end(k):
        first, size, h, r = shape_of(k)
        if h:
            arrive(("gs", k), speed[k].at[pl.ds((1 - y) * r, h)])

    def step_one(k):
        first, size, h, r = shape_of(k)
        gather_end(k)

        def body(layer, inside):
            npad[pl.ds(layer + HALO, 4)] = (base[pl.ds(layer, 4)]
                                            + speed[k][pl.ds(inside, 4)] * lap[pl.ds(layer, 4)])

        groups(k, body)
        local(("prior", k), npad.at[pl.ds(HALO + first, size)], prior_out.at[0, pl.ds(first, size)])

    def step_two(k):
        first, size, h, r = shape_of(k)
        if k == 0:
            halo_low(second_halo)
        if k == len(CHUNKS) - 1:
            halo_high(second_halo)
        if k == first_two:
            locals_["snap"].wait()

        def body(layer, inside):
            field, summed = laplace(npad, layer)
            value = (2.0 * field - fpad[pl.ds(layer + HALO, 4)] + speed[k][pl.ds(inside, 4)] * summed
                     + injected(layer, 1).reshape(4, NY, NZ))
            last[pl.ds(layer, 4)] = value
            seen = snap[0, pl.ds(layer, 4)].astype(F32) * field + snap[1, pl.ds(layer, 4)].astype(F32) * value
            for j in range(4):
                img[k][j, pl.ds(inside, 4)] = seen[:, BY * j:BY * j + BY, :]

        groups(k, body)
        local(("final", k), last.at[pl.ds(first, size)], final_out.at[0, pl.ds(first, size)])
        img[k][4] = jnp.zeros((size, BY, NZ), F32)
        if h:
            imgin[k][4] = jnp.zeros((h, BY, NZ), F32)
            send(("ry", k), img[k].at[pl.ds(0, 4), pl.ds((1 - y) * r, h)], imgin[k].at[pl.ds(0, 4)], "Y")

    def place(first_block, storage):
        block = block_of[storage] - first_block
        return jnp.where((block >= 0) & (block < 4), block, 4)

    def reduce_sibling(k):
        first, size, h, r = shape_of(k)
        if h:
            arrive(("ry", k), imgin[k].at[pl.ds(0, 4)])
        for to, core in ((sibout[k], 1 - c), (acc[k], c)):
            def body(slot, carry, to=to, core=core):
                storage = 2 * slot + core
                to[slot] = img[k][place(my_first, storage), pl.ds(y * h, r)]
                if h:
                    inner = pl.ds(y * (r - h), h)
                    to[slot, inner] = to[slot, inner] + imgin[k][place(their_first, storage)]
                return carry

            lax.fori_loop(0, 8, body, 0)
            if to is sibout[k]:
                send(("rc", k), sibout[k], sibin[k], "C")

    def reduce_x(k):
        arrive(("rc", k), sibin[k])

        def body(slot, carry):
            acc[k][slot] = acc[k][slot] + sibin[k][slot]
            return carry

        lax.fori_loop(0, 8, body, 0)
        for i, row in enumerate((1 - y, y)):
            send(("rd", i, k), acc[k].at[2 * column(D, way) + row], xin[k].at[i], "B")
            send(("ra", i, k), acc[k].at[2 * column(A, way) + row], xin[k].at[2 + i], "A")

    def reduce_forward(k, i, row):
        arrive(("rd", i, k), xin[k].at[i])
        to_b = 2 * column(B, way) + row
        acc[k][to_b] = acc[k][to_b] + xin[k][i]
        send(("rb", i, k), acc[k].at[to_b], xin[k].at[4 + i], "B")

    def reduce_theirs(k):
        reduce_forward(k, 0, 1 - y)

    def reduce_ours(k):
        reduce_forward(k, 1, y)

    def collected(k, i, row):
        arrive(("ra", i, k), xin[k].at[2 + i])
        arrive(("rb", i, k), xin[k].at[4 + i])
        return acc[k][2 * x + row] + xin[k][2 + i] + xin[k][4 + i]

    def reduce_y(k):
        acc[k][2 * x + 1 - y] = collected(k, 0, 1 - y)
        send(("rz", k), acc[k].at[2 * x + 1 - y], yin[k], "Y")

    def finish(k):
        first, size, h, r = shape_of(k)
        if h:
            imgout[k][...] = jnp.zeros((size, BY, NZ), F32)
        imgout[k][pl.ds(y * h, r)] = collected(k, 1, y)
        arrive(("rz", k), yin[k])
        theirs = pl.ds((1 - y) * h, r)
        imgout[k][theirs] = imgout[k][theirs] + yin[k][...]
        local(("image", k), imgout[k], image_out.at[pl.ds(first, size)])

    for k in ORDER:
        gather_y(k)
    first_halo = []
    second_halo = []

    def first_edges(k):
        @pl.when(c == 1)
        def _():
            pl.semaphore_wait(barrier, 2)
            tell(inside_sub, "C")

        @pl.when(c == 0)
        def _():
            pl.semaphore_wait(inside_sub, 1)

        first_halo.extend(halo_send("h0", now.at[0, pl.ds(NX - HALO, HALO)], now.at[0, pl.ds(0, HALO)], fpad))

    for name in ("traces", "receivers", "aperture", "block_of"):
        locals_[name].wait()
    my_first = aperture[s]
    their_first = aperture[(x * 2 + 1 - y) * 2 + c]
    my_slots = slots_from(my_first)
    their_slots = slots_from(their_first)

    def constants(k):
        @pl.when(u == 0)
        def _():
            fpad[0:HALO] = jnp.zeros((HALO, NY, NZ), F32)
            npad[0:HALO] = jnp.zeros((HALO, NY, NZ), F32)

        @pl.when(u == 15)
        def _():
            fpad[HALO + NX:] = jnp.zeros((HALO, NY, NZ), F32)
            npad[HALO + NX:] = jnp.zeros((HALO, NY, NZ), F32)

        matrices()
        depth_spots()
        for j in range(len(CHUNKS)):
            locals_[("now", j)].wait()

    def edges(k):
        second_halo.extend(halo_send("h1", npad.at[pl.ds(NX, HALO)], npad.at[pl.ds(HALO, HALO)], npad))

    steps = {
        "o": gather_own, "x": gather_x, "a": gather_a, "b": gather_b, "d": gather_d, "s": gather_stage,
        "Z": first_edges, "M": constants, "P": prepare, "1": step_one, "H": edges, "2": step_two,
        "p": reduce_sibling, "q": reduce_x, "r": reduce_theirs, "R": reduce_ours, "t": reduce_y, "f": finish,
    }
    for name in SEQUENCE:
        steps[name[0]](int(name[1:]))

    halo_sent(first_halo)
    halo_sent(second_halo)
    for copy in sent:
        copy.wait_send()
    for name in locals_:
        if name[0] in ("prior", "final", "image"):
            locals_[name].wait()


def hand_on(prior, final, image, prior_out, final_out, image_out, prior_held, final_held, image_held,
            in_sems, out_sems):
    pieces = []
    for piece in range(4):
        rows = pl.ds(8 * piece, 8)
        pieces.append((prior.at[0, rows], prior_held.at[rows], prior_out.at[0, rows]))
        pieces.append((final.at[0, rows], final_held.at[rows], final_out.at[0, rows]))
    pieces.append((image, image_held, image_out))
    loads = [pltpu.make_async_copy(src, held, in_sems.at[i]) for i, (src, held, dst) in enumerate(pieces)]
    stores = [pltpu.make_async_copy(held, dst, out_sems.at[i]) for i, (src, held, dst) in enumerate(pieces)]
    for load in loads:
        load.start()
    for load, store in zip(loads, stores):
        load.wait()
        store.start()
    for store in stores:
        store.wait()


def local(field_before, field_now, snapshots, traces, receivers, courant, aperture, block_of):
    anywhere = pl.BlockSpec(memory_space=pl.ANY)

    def per_chunk(dims):
        return [pltpu.VMEM(dims(size, h, size - h), F32) for first, size, h in CHUNKS]

    field = (NX, NY, NZ)
    padded = (NX + 2 * HALO, NY, NZ)
    block = (BY, NZ)
    count = 24 * len(CHUNKS) + 8
    scratch = [
        pltpu.VMEM(traces.shape, F32), pltpu.VMEM(receivers.shape, jnp.int32),
        pltpu.SMEM(aperture.shape, jnp.int32), pltpu.SMEM(block_of.shape, jnp.int32),
        pltpu.VMEM(padded, F32), pltpu.VMEM(padded, F32),
        pltpu.VMEM(field, F32), pltpu.VMEM(field, F32), pltpu.VMEM(field, F32),
        pltpu.VMEM((2,) + field, BF16),
        pltpu.VMEM((768, 256), BF16), pltpu.VMEM((256, 768), BF16),
        pltpu.VMEM((2, NZ, 3 * NR), BF16),
        per_chunk(lambda n, h, r: (n, NY, NZ)),
        per_chunk(lambda n, h, r: (NB, r) + block),
        per_chunk(lambda n, h, r: (max(h, 1), NY, NZ)),
        per_chunk(lambda n, h, r: (5, n) + block),
        per_chunk(lambda n, h, r: (5, max(h, 1)) + block),
        per_chunk(lambda n, h, r: (8, r) + block),
        per_chunk(lambda n, h, r: (8, r) + block),
        per_chunk(lambda n, h, r: (8, r) + block),
        per_chunk(lambda n, h, r: (6, r) + block),
        per_chunk(lambda n, h, r: (r,) + block),
        per_chunk(lambda n, h, r: (n,) + block),
        pltpu.SemaphoreType.DMA((count,)),
        pltpu.SemaphoreType.DMA((count,)),
        pltpu.SemaphoreType.DMA((8 * len(CHUNKS),)),
        pltpu.SemaphoreType.REGULAR,
        pltpu.SemaphoreType.REGULAR,
    ]
    results = pl.pallas_call(
        kernel,
        out_shape=(
            jax.ShapeDtypeStruct(field_now.shape, F32),
            jax.ShapeDtypeStruct(field_now.shape, F32),
            jax.ShapeDtypeStruct(courant.shape, F32),
        ),
        in_specs=[pl.BlockSpec(memory_space=pltpu.HBM)] * 8,
        out_specs=(anywhere, anywhere, anywhere),
        scratch_shapes=scratch,
        compiler_params=pltpu.CompilerParams(
            collective_id=0, has_side_effects=True, vmem_limit_bytes=60 << 20),
    )(field_before, field_now, snapshots, traces, receivers, courant, aperture, block_of)
    return pl.pallas_call(
        hand_on,
        out_shape=tuple(jax.ShapeDtypeStruct(result.shape, F32) for result in results),
        in_specs=[pl.BlockSpec(memory_space=pltpu.HBM)] * 3,
        out_specs=(pl.BlockSpec(memory_space=pltpu.HBM),) * 3,
        scratch_shapes=[
            pltpu.VMEM(results[0].shape[1:], F32), pltpu.VMEM(results[1].shape[1:], F32),
            pltpu.VMEM(results[2].shape, F32),
            pltpu.SemaphoreType.DMA((9,)), pltpu.SemaphoreType.DMA((9,)),
        ],
        compiler_params=pltpu.CompilerParams(vmem_limit_bytes=60 << 20),
    )(*results)


def solution(mesh):
    in_specs = (
        P("shot", "sub", None, None),
        P("shot", "sub", None, None),
        P("shot", None, "sub", None, None),
        P("shot", "sub", None, None),
        P("shot", "sub", None),
        P("sub", "shot", None),
        P(),
        P(),
    )
    out_specs = (P("shot", "sub", None, None), P("shot", "sub", None, None), P("sub", "shot", None))
    return jax.shard_map(local, mesh=mesh, in_specs=in_specs, out_specs=out_specs, check_vma=False)
```

```python
import functools

import jax
import jax.numpy as jnp
import ml_dtypes
import numpy as np
from jax import lax
from jax.experimental import pallas as pl
from jax.experimental.pallas import tpu as pltpu
from jax.sharding import PartitionSpec as P

MESH = pl.DeviceIdType.MESH
F32 = jnp.float32
BF16 = jnp.bfloat16

NX, NY, NZ, BY, NB, NR = 32, 64, 256, 16, 16, 128
HALO = 4
centre_weight = -205.0 / 72.0
side_weights = (8.0 / 5.0, -1.0 / 5.0, 8.0 / 315.0, -1.0 / 560.0)

CHUNKS = ((0, 4, 2), (4, 4, 0), (8, 4, 2), (12, 4, 0), (16, 4, 1), (20, 4, 2), (24, 4, 2), (28, 4, 0))
ORDER = (7, 0, 1, 2, 3, 4, 5, 6)
LOADS = tuple(range(1, len(CHUNKS) - 1)) + (0, len(CHUNKS) - 1)
SEQUENCE = (
    "o7", "o0", "M0", "o5", "o2", "x0", "x7", "Z0", "x2", "o1", "a0", "P4", "a7", "b0",
    "a2", "P2", "o4", "x4", "b2", "d0", "o3", "s0", "o6", "x6", "x5", "d2", "b7", "x1",
    "s2", "d7", "P0", "P7", "a4", "x3", "s7", "17", "10", "H0", "a6", "b6", "P3", "b1",
    "b4", "a1", "d4", "b5", "a5", "a3", "12", "s4", "d6", "d1", "s6", "d5", "b3", "P1",
    "s1", "d3", "11", "s5", "21", "p1", "14", "s3", "13", "23", "p3", "22", "P6", "q1",
    "P5", "16", "27", "q3", "p7", "15", "26", "24", "r1", "20", "25", "r3", "q7", "p2",
    "q2", "p6", "r7", "p4", "q6", "p0", "t3", "r2", "q4", "q0", "p5", "t7", "t1", "r4",
    "q5", "r0", "t2", "r6", "R3", "r5", "R0", "t4", "R4", "R1", "R6", "t0", "t6", "R2",
    "R7", "t5", "R5", "f1", "f3", "f2", "f6", "f4", "f0", "f7", "f5",
)
OWN, A, B, D = range(4)


def split(value):
    high = value.astype(BF16)
    low = (value - high.astype(F32)).astype(BF16)
    return high, low


def band(i, j):
    apart = jnp.abs(i - j)
    high = jnp.zeros(apart.shape, F32)
    low = jnp.zeros(apart.shape, F32)
    for distance in range(1, 5):
        weight = np.float32(side_weights[distance - 1])
        top = np.float32(weight.astype(ml_dtypes.bfloat16))
        high = jnp.where(apart == distance, float(top), high)
        low = jnp.where(apart == distance, float(weight - top), low)
    return high.astype(BF16), low.astype(BF16)


def kernel(before, now, snapshots, traces_in, receivers_in, courant, aperture_in, block_of_in,
           prior_out, final_out, image_out,
           traces, receivers, aperture, block_of, fpad, npad, base, lap, last, snap, wz, wy, spots,
           speed, gath, stage, img, imgin, sibout, sibin, acc, xin, yin, imgout,
           send_sems, recv_sems, local_sems, inside, inside_sub):
    s = lax.axis_index("shot")
    u = lax.axis_index("sub")
    c = lax.rem(s, 2)
    y = lax.rem(s // 2, 2)
    x = s // 4
    way = 1 - 2 * c

    def at(x_, y_, c_):
        return {"shot": (x_ * 2 + y_) * 2 + c_, "sub": u}

    def column(role, way_):
        return lax.rem({OWN: x, A: x - way_ + 4, B: x + way_ + 4, D: x + 2}[role], 4)

    dev = {
        "A": at(column(A, way), y, c),
        "B": at(column(B, way), y, c),
        "Y": at(x, 1 - y, c),
        "C": at(x, y, 1 - c),
        "S+": {"shot": s, "sub": lax.rem(u + 1, 16)},
        "S-": {"shot": s, "sub": lax.rem(u + 15, 16)},
    }
    barrier = pltpu.get_barrier_semaphore()

    def tell(semaphore, name):
        pl.semaphore_signal(semaphore, inc=1, device_id=dev[name], device_id_type=MESH)

    @pl.when(c == 0)
    def _():
        for name in "ABY":
            tell(barrier, name)

    @pl.when(c == 1)
    def _():
        tell(barrier, "C")

    first_two = [int(name[1:]) for name in SEQUENCE if name[0] == "2"][0]
    ids = {}
    sent = []

    def number(name):
        return ids.setdefault(name, len(ids))

    def copy_of(name, src, dst, to):
        n = number(name)
        return pltpu.make_async_remote_copy(
            src_ref=src, dst_ref=dst, send_sem=send_sems.at[n], recv_sem=recv_sems.at[n],
            device_id=dev[to], device_id_type=MESH)

    def send(name, src, dst, to):
        copy = copy_of(name, src, dst, to)
        copy.start()
        sent.append(copy)

    def arrive(name, dst):
        copy_of(name, dst, dst, "Y").wait_recv()

    locals_ = {}

    def local(name, src, dst):
        copy = pltpu.make_async_copy(src, dst, local_sems.at[len(locals_)])
        locals_[name] = copy
        copy.start()

    def shape_of(k):
        first, size, h = CHUNKS[k]
        return first, size, h, size - h

    for k in ORDER:
        first, size, h, r = shape_of(k)
        local(("own", k), courant.at[pl.ds(first + y * h, r)], gath[k].at[c * 8 + x * 2 + y])
    for k in LOADS:
        first, size, h, r = shape_of(k)
        local(("now", k), now.at[0, pl.ds(first, size)], fpad.at[pl.ds(HALO + first, size)])
    for k in LOADS:
        first, size, h, r = shape_of(k)
        local(("before", k), before.at[0, pl.ds(first, size)], base.at[pl.ds(first, size)])
    local("snap", snapshots.at[0], snap)
    for name, src, dst in (("traces", traces_in, traces), ("receivers", receivers_in, receivers),
                           ("aperture", aperture_in, aperture), ("block_of", block_of_in, block_of)):
        local(name, src, dst)

    @pl.when(c == 0)
    def _():
        pl.semaphore_wait(barrier, 4)
        for name in "ABY":
            tell(inside, name)
        pl.semaphore_wait(inside, 3)
        tell(inside, "C")

    @pl.when(c == 1)
    def _():
        pl.semaphore_wait(inside, 1)
        tell(barrier, "S+")
        tell(barrier, "S-")


    def halo_send(name, up_src, down_src, pad):
        up = copy_of(name + "up", up_src, pad.at[pl.ds(0, HALO)], "S+")
        down = copy_of(name + "down", down_src, pad.at[pl.ds(HALO + NX, HALO)], "S-")

        @pl.when(u < 15)
        def _():
            up.start()

        @pl.when(u > 0)
        def _():
            down.start()

        return up, down

    def halo_low(copies):
        @pl.when(u > 0)
        def _():
            copies[0].wait_recv()

    def halo_high(copies):
        @pl.when(u < 15)
        def _():
            copies[1].wait_recv()

    def halo_sent(copies):
        @pl.when(u < 15)
        def _():
            copies[0].wait_send()

        @pl.when(u > 0)
        def _():
            copies[1].wait_send()

    def pair(role, c_):
        return pl.ds(c_ * 8 + 2 * column(role, 1 - 2 * c_), 2)

    def gather_y(k):
        first, size, h, r = shape_of(k)
        send(("gy", k), courant.at[pl.ds(first + (1 - y) * h, r)], gath[k].at[c * 8 + x * 2 + y], "Y")

    def gather_own(k):
        locals_[("own", k)].wait()
        mine = gath[k].at[c * 8 + x * 2 + y]
        send(("ga", 0, k), mine, mine, "A")
        send(("gb", 0, k), mine, mine, "B")

    def gather_x(k):
        theirs = gath[k].at[c * 8 + x * 2 + 1 - y]
        arrive(("gy", k), theirs)
        send(("ga", 1, k), theirs, theirs, "A")
        send(("gb", 1, k), theirs, theirs, "B")
        both = gath[k].at[pair(OWN, c)]
        send(("gc", OWN, k), both, both, "C")

    def gather_a(k):
        column_a = column(A, way)
        arrive(("gb", 0, k), gath[k].at[c * 8 + 2 * column_a + y])
        arrive(("gb", 1, k), gath[k].at[c * 8 + 2 * column_a + 1 - y])
        both = gath[k].at[pair(A, c)]
        send(("gd", k), both, both, "B")
        send(("gc", A, k), both, both, "C")

    def gather_b(k):
        column_b = column(B, way)
        arrive(("ga", 0, k), gath[k].at[c * 8 + 2 * column_b + y])
        arrive(("ga", 1, k), gath[k].at[c * 8 + 2 * column_b + 1 - y])
        both = gath[k].at[pair(B, c)]
        send(("gc", B, k), both, both, "C")

    def gather_d(k):
        both = gath[k].at[pair(D, c)]
        arrive(("gd", k), both)
        send(("gc", D, k), both, both, "C")

    def slots_from(first_block):
        found = []
        for j in range(4):
            slot = 0
            for b in range(NB):
                slot = jnp.where(block_of[b] == first_block + j, (b % 2) * 8 + b // 2, slot)
            found.append(slot)
        return found

    def gather_stage(k):
        first, size, h, r = shape_of(k)
        for role in (OWN, A, B, D):
            arrive(("gc", role, k), gath[k].at[pair(role, 1 - c)])
        for j in range(4 if h else 0):
            stage[k][:, BY * j:BY * j + BY, :] = gath[k][their_slots[j], pl.ds(y * (r - h), h)]
        if h:
            send(("gs", k), stage[k], speed[k].at[pl.ds(y * r, h)], "Y")
        for j in range(4):
            speed[k][pl.ds(y * h, r), BY * j:BY * j + BY, :] = gath[k][my_slots[j]]

    def matrices():
        i = lax.broadcasted_iota(jnp.int32, (256, 256), 0)
        j = lax.broadcasted_iota(jnp.int32, (256, 256), 1)
        high, low = band(i, j)
        wz[0:256, :] = high
        wz[256:512, :] = high
        wz[512:768, :] = low
        same = (i // NY) == (j // NY)
        high = jnp.where(same, high.astype(F32), 0.0).astype(BF16)
        low = jnp.where(same, low.astype(F32), 0.0).astype(BF16)
        wy[:, 0:256] = high
        wy[:, 256:512] = high
        wy[:, 512:768] = low

    def depth_spots():
        z = lax.broadcasted_iota(jnp.int32, (NZ, NR), 0)
        at_depth = z == lax.rem(receivers[0], NZ)
        for t in range(2):
            value = jnp.where(at_depth, traces[0, 0, t:t + 1, :], 0.0)
            high = value.astype(BF16)
            rest = value - high.astype(F32)
            middle = rest.astype(BF16)
            low = (rest - middle.astype(F32)).astype(BF16)
            spots[t, :, 0:NR] = high
            spots[t, :, NR:2 * NR] = middle
            spots[t, :, 2 * NR:3 * NR] = low

    def injected(layer, t):
        row = lax.broadcasted_iota(jnp.int32, (4 * NY, NR), 0) + layer * NY
        hit = jnp.where(row == receivers[0] // NZ, 1.0, 0.0).astype(BF16)
        hits = jnp.concatenate([hit, hit, hit], axis=1)
        return lax.dot_general(hits, spots[t], (((1,), (1,)), ((), ())), preferred_element_type=F32)

    def laplace(pad, layer):
        field = pad[pl.ds(layer + HALO, 4)]
        rows = field.reshape(4 * NY, NZ)
        high, low = split(rows)
        summed = jnp.dot(jnp.concatenate([high, low, high], axis=1), wz[...], preferred_element_type=F32)
        summed = summed + jnp.dot(wy[...], jnp.concatenate([high, low, high], axis=0), preferred_element_type=F32)
        summed = summed.reshape(4, NY, NZ) + (3.0 * centre_weight) * field
        for distance in range(1, 5):
            summed = summed + side_weights[distance - 1] * (
                pad[pl.ds(layer + HALO + distance, 4)] + pad[pl.ds(layer + HALO - distance, 4)])
        return field, summed

    def groups(k, body):
        first, size, h, r = shape_of(k)

        if size == 4:
            body(first, 0)
            return

        def step(g, carry):
            body(first + 4 * g, 4 * g)
            return carry

        lax.fori_loop(0, size // 4, step, 0)

    def prepare(k):
        if k == 0:
            halo_low(first_halo)
        if k == len(CHUNKS) - 1:
            halo_high(first_halo)
        locals_[("before", k)].wait()

        def body(layer, inside):
            field, summed = laplace(fpad, layer)
            lap[pl.ds(layer, 4)] = summed
            base[pl.ds(layer, 4)] = (2.0 * field - base[pl.ds(layer, 4)]
                                     + injected(layer, 0).reshape(4, NY, NZ))

        groups(k, body)

    def gather_end(k):
        first, size, h, r = shape_of(k)
        if h:
            arrive(("gs", k), speed[k].at[pl.ds((1 - y) * r, h)])

    def step_one(k):
        first, size, h, r = shape_of(k)
        gather_end(k)

        def body(layer, inside):
            npad[pl.ds(layer + HALO, 4)] = (base[pl.ds(layer, 4)]
                                            + speed[k][pl.ds(inside, 4)] * lap[pl.ds(layer, 4)])

        groups(k, body)
        local(("prior", k), npad.at[pl.ds(HALO + first, size)], prior_out.at[0, pl.ds(first, size)])

    def step_two(k):
        first, size, h, r = shape_of(k)
        if k == 0:
            halo_low(second_halo)
        if k == len(CHUNKS) - 1:
            halo_high(second_halo)
        if k == first_two:
            locals_["snap"].wait()

        def body(layer, inside):
            field, summed = laplace(npad, layer)
            value = (2.0 * field - fpad[pl.ds(layer + HALO, 4)] + speed[k][pl.ds(inside, 4)] * summed
                     + injected(layer, 1).reshape(4, NY, NZ))
            last[pl.ds(layer, 4)] = value
            seen = snap[0, pl.ds(layer, 4)].astype(F32) * field + snap[1, pl.ds(layer, 4)].astype(F32) * value
            for j in range(4):
                img[k][j, pl.ds(inside, 4)] = seen[:, BY * j:BY * j + BY, :]

        groups(k, body)
        local(("final", k), last.at[pl.ds(first, size)], final_out.at[0, pl.ds(first, size)])
        img[k][4] = jnp.zeros((size, BY, NZ), F32)
        if h:
            imgin[k][4] = jnp.zeros((h, BY, NZ), F32)
            send(("ry", k), img[k].at[pl.ds(0, 4), pl.ds((1 - y) * r, h)], imgin[k].at[pl.ds(0, 4)], "Y")

    def place(first_block, storage):
        block = block_of[storage] - first_block
        return jnp.where((block >= 0) & (block < 4), block, 4)

    def reduce_sibling(k):
        first, size, h, r = shape_of(k)
        if h:
            arrive(("ry", k), imgin[k].at[pl.ds(0, 4)])
        for to, core in ((sibout[k], 1 - c), (acc[k], c)):
            def body(slot, carry, to=to, core=core):
                storage = 2 * slot + core
                to[slot] = img[k][place(my_first, storage), pl.ds(y * h, r)]
                if h:
                    inner = pl.ds(y * (r - h), h)
                    to[slot, inner] = to[slot, inner] + imgin[k][place(their_first, storage)]
                return carry

            lax.fori_loop(0, 8, body, 0)
            if to is sibout[k]:
                send(("rc", k), sibout[k], sibin[k], "C")

    def reduce_x(k):
        arrive(("rc", k), sibin[k])

        def add(role, row):
            slot = 2 * column(role, way) + row
            acc[k][slot] = acc[k][slot] + sibin[k][slot]
            return acc[k].at[slot]

        for i, row in enumerate((1 - y, y)):
            send(("rd", i, k), add(D, row), xin[k].at[i], "B")
            send(("ra", i, k), add(A, row), xin[k].at[2 + i], "A")
        for role in (B, OWN):
            for row in (1 - y, y):
                add(role, row)

    def reduce_forward(k, i, row):
        arrive(("rd", i, k), xin[k].at[i])
        to_b = 2 * column(B, way) + row
        acc[k][to_b] = acc[k][to_b] + xin[k][i]
        send(("rb", i, k), acc[k].at[to_b], xin[k].at[4 + i], "B")

    def reduce_theirs(k):
        reduce_forward(k, 0, 1 - y)

    def reduce_ours(k):
        reduce_forward(k, 1, y)

    def collected(k, i, row):
        arrive(("ra", i, k), xin[k].at[2 + i])
        arrive(("rb", i, k), xin[k].at[4 + i])
        return acc[k][2 * x + row] + xin[k][2 + i] + xin[k][4 + i]

    def reduce_y(k):
        acc[k][2 * x + 1 - y] = collected(k, 0, 1 - y)
        send(("rz", k), acc[k].at[2 * x + 1 - y], yin[k], "Y")

    def finish(k):
        first, size, h, r = shape_of(k)
        if h:
            imgout[k][...] = jnp.zeros((size, BY, NZ), F32)
        imgout[k][pl.ds(y * h, r)] = collected(k, 1, y)
        arrive(("rz", k), yin[k])
        theirs = pl.ds((1 - y) * h, r)
        imgout[k][theirs] = imgout[k][theirs] + yin[k][...]
        local(("image", k), imgout[k], image_out.at[pl.ds(first, size)])

    for k in ORDER:
        gather_y(k)
    first_halo = []
    second_halo = []

    def first_edges(k):
        @pl.when(c == 1)
        def _():
            pl.semaphore_wait(barrier, 2)
            tell(inside_sub, "C")

        @pl.when(c == 0)
        def _():
            pl.semaphore_wait(inside_sub, 1)

        first_halo.extend(halo_send("h0", now.at[0, pl.ds(NX - HALO, HALO)], now.at[0, pl.ds(0, HALO)], fpad))

    for name in ("traces", "receivers", "aperture", "block_of"):
        locals_[name].wait()
    my_first = aperture[s]
    their_first = aperture[(x * 2 + 1 - y) * 2 + c]
    my_slots = slots_from(my_first)
    their_slots = slots_from(their_first)

    def constants(k):
        @pl.when(u == 0)
        def _():
            fpad[0:HALO] = jnp.zeros((HALO, NY, NZ), F32)
            npad[0:HALO] = jnp.zeros((HALO, NY, NZ), F32)

        @pl.when(u == 15)
        def _():
            fpad[HALO + NX:] = jnp.zeros((HALO, NY, NZ), F32)
            npad[HALO + NX:] = jnp.zeros((HALO, NY, NZ), F32)

        matrices()
        depth_spots()
        for j in range(len(CHUNKS)):
            locals_[("now", j)].wait()

    def edges(k):
        second_halo.extend(halo_send("h1", npad.at[pl.ds(NX, HALO)], npad.at[pl.ds(HALO, HALO)], npad))

    steps = {
        "o": gather_own, "x": gather_x, "a": gather_a, "b": gather_b, "d": gather_d, "s": gather_stage,
        "Z": first_edges, "M": constants, "P": prepare, "1": step_one, "H": edges, "2": step_two,
        "p": reduce_sibling, "q": reduce_x, "r": reduce_theirs, "R": reduce_ours, "t": reduce_y, "f": finish,
    }
    for name in SEQUENCE:
        steps[name[0]](int(name[1:]))

    halo_sent(first_halo)
    halo_sent(second_halo)
    for copy in sent:
        copy.wait_send()
    for name in locals_:
        if name[0] in ("prior", "final", "image"):
            locals_[name].wait()


def hand_on(prior, final, image, prior_out, final_out, image_out, prior_held, final_held, image_held,
            in_sems, out_sems):
    pieces = []
    for piece in range(4):
        rows = pl.ds(8 * piece, 8)
        pieces.append((prior.at[0, rows], prior_held.at[rows], prior_out.at[0, rows]))
        pieces.append((final.at[0, rows], final_held.at[rows], final_out.at[0, rows]))
    pieces.append((image, image_held, image_out))
    loads = [pltpu.make_async_copy(src, held, in_sems.at[i]) for i, (src, held, dst) in enumerate(pieces)]
    stores = [pltpu.make_async_copy(held, dst, out_sems.at[i]) for i, (src, held, dst) in enumerate(pieces)]
    for load in loads:
        load.start()
    for load, store in zip(loads, stores):
        load.wait()
        store.start()
    for store in stores:
        store.wait()


def local(field_before, field_now, snapshots, traces, receivers, courant, aperture, block_of):
    anywhere = pl.BlockSpec(memory_space=pl.ANY)

    def per_chunk(dims):
        return [pltpu.VMEM(dims(size, h, size - h), F32) for first, size, h in CHUNKS]

    field = (NX, NY, NZ)
    padded = (NX + 2 * HALO, NY, NZ)
    block = (BY, NZ)
    count = 24 * len(CHUNKS) + 8
    scratch = [
        pltpu.VMEM(traces.shape, F32), pltpu.VMEM(receivers.shape, jnp.int32),
        pltpu.SMEM(aperture.shape, jnp.int32), pltpu.SMEM(block_of.shape, jnp.int32),
        pltpu.VMEM(padded, F32), pltpu.VMEM(padded, F32),
        pltpu.VMEM(field, F32), pltpu.VMEM(field, F32), pltpu.VMEM(field, F32),
        pltpu.VMEM((2,) + field, BF16),
        pltpu.VMEM((768, 256), BF16), pltpu.VMEM((256, 768), BF16),
        pltpu.VMEM((2, NZ, 3 * NR), BF16),
        per_chunk(lambda n, h, r: (n, NY, NZ)),
        per_chunk(lambda n, h, r: (NB, r) + block),
        per_chunk(lambda n, h, r: (max(h, 1), NY, NZ)),
        per_chunk(lambda n, h, r: (5, n) + block),
        per_chunk(lambda n, h, r: (5, max(h, 1)) + block),
        per_chunk(lambda n, h, r: (8, r) + block),
        per_chunk(lambda n, h, r: (8, r) + block),
        per_chunk(lambda n, h, r: (8, r) + block),
        per_chunk(lambda n, h, r: (6, r) + block),
        per_chunk(lambda n, h, r: (r,) + block),
        per_chunk(lambda n, h, r: (n,) + block),
        pltpu.SemaphoreType.DMA((count,)),
        pltpu.SemaphoreType.DMA((count,)),
        pltpu.SemaphoreType.DMA((8 * len(CHUNKS),)),
        pltpu.SemaphoreType.REGULAR,
        pltpu.SemaphoreType.REGULAR,
    ]
    results = pl.pallas_call(
        kernel,
        out_shape=(
            jax.ShapeDtypeStruct(field_now.shape, F32),
            jax.ShapeDtypeStruct(field_now.shape, F32),
            jax.ShapeDtypeStruct(courant.shape, F32),
        ),
        in_specs=[pl.BlockSpec(memory_space=pltpu.HBM)] * 8,
        out_specs=(anywhere, anywhere, anywhere),
        scratch_shapes=scratch,
        compiler_params=pltpu.CompilerParams(
            collective_id=0, has_side_effects=True, vmem_limit_bytes=60 << 20),
    )(field_before, field_now, snapshots, traces, receivers, courant, aperture, block_of)
    return pl.pallas_call(
        hand_on,
        out_shape=tuple(jax.ShapeDtypeStruct(result.shape, F32) for result in results),
        in_specs=[pl.BlockSpec(memory_space=pltpu.HBM)] * 3,
        out_specs=(pl.BlockSpec(memory_space=pltpu.HBM),) * 3,
        scratch_shapes=[
            pltpu.VMEM(results[0].shape[1:], F32), pltpu.VMEM(results[1].shape[1:], F32),
            pltpu.VMEM(results[2].shape, F32),
            pltpu.SemaphoreType.DMA((9,)), pltpu.SemaphoreType.DMA((9,)),
        ],
        compiler_params=pltpu.CompilerParams(vmem_limit_bytes=60 << 20),
    )(*results)


def solution(mesh):
    in_specs = (
        P("shot", "sub", None, None),
        P("shot", "sub", None, None),
        P("shot", None, "sub", None, None),
        P("shot", "sub", None, None),
        P("shot", "sub", None),
        P("sub", "shot", None),
        P(),
        P(),
    )
    out_specs = (P("shot", "sub", None, None), P("shot", "sub", None, None), P("sub", "shot", None))
    return jax.shard_map(local, mesh=mesh, in_specs=in_specs, out_specs=out_specs, check_vma=False)
```
